32 devices in a mesh: sub: 8 (over z, x), vec: 4 (over y, core).
Axes of the slice: x: 2, y: 2, z: 4, core: 2. Of those that a mesh axis runs over, the one named last changes fastest.
Arguments:
- coefficients: bfloat16 [1024, 5120], P('sub', 'vec'), may hold values from -6 to 6
- row_counts: int32 [8], replicated, may hold values from 1 to 1024, 4096 in all
- ancestors: int32 [8, 3], replicated, may hold values from 0 to 6, as said below
- interior_modes: bfloat16 [32768, 1024], P('sub'), may hold values from -0.25 to 0.25
- separator_modes: bfloat16 [2048, 128], replicated, may hold values from -0.5 to 0.5
- coupling: bfloat16 [32768, 768], P('sub'), may hold values from -0.3125 to 0.3125
- pattern: int32 [8, 16, 3], P('sub'), may hold values 0 or 1
Outputs:
- interior_field: bfloat16 [32768, 1024], P('sub', 'vec')
- separator_field: bfloat16 [2048, 1024], P('sub', 'vec')
The draws below stay inside these ranges and needn't reach their ends.
Inputs may be any that keep to these rules, and one draw needn't show every extreme that they name: `ancestors`: the separators form binary trees: substructures pair under level-1 separators, pairs of those under level-2 separators, and so on, so that a level-l separator lies over 2**l substructures; no separator appears at two levels. `row_counts`: the counts sum to 512 * 8.
All inputs are finite; a program needn't handle non-finite values. No bound on the sum of `pattern` on one device may be relied on, other than what follows from the above.
Results may differ from the reference program's by a relative error of at most 0.0038.
Values may be sent and summed in bfloat16 or wider, within the bound.
No kernel may reach another device: no remote copies, remote signals or barrier semaphores. Data moves between devices by JAX's collectives and lax.ppermute only.
A program may use at most 128 MiB of HBM per device.

```python
import math
import jax
import jax.numpy as jnp
import numpy as np
from jax import lax

K = 1024
BW = 256
SEPM = 128
LEVELS = 3
ROWS_MEAN = 512
PHYS = 4096
CAP = 1024
NBLK = 16
M = 5120
N_SUB = 8
N_VEC = 4


def draw_ancestors(key, part):
    leaf_place = jax.random.permutation(jax.random.fold_in(key, 11), N_SUB)
    labels = jax.random.permutation(jax.random.fold_in(key, 12), 7 * N_SUB // 8)
    level_one = labels[leaf_place // 2]
    level_two = labels[N_SUB // 2 + leaf_place // 4]
    level_three = labels[3 * N_SUB // 4 + leaf_place // 8]
    return jnp.stack([level_one, level_two, level_three], axis=1).astype(jnp.int32)


def touch_ends(array, own_key, smallest, top_value):
    longest = array.shape.index(max(array.shape))
    spots = []
    for shift in (0, 1):
        where = [jax.random.randint(jax.random.fold_in(own_key, axis), (), 0, length) for axis, length in enumerate(array.shape)]
        where[longest] = (where[longest] + shift) % array.shape[longest]
        spots.append(tuple(where))
    return array.at[spots[0]].set(smallest).at[spots[1]].set(top_value)


def block_scale(own_key, dims, split, smallest, high):
    def one(dim, blocks):
        heights = jax.random.uniform(jax.random.fold_in(jax.random.fold_in(own_key, 6), dim), (blocks,), jnp.float32, smallest / len(split), high / len(split))
        return jnp.repeat(jnp.exp(heights), dims[dim] // blocks).reshape((-1,) + (1,) * (len(dims) - dim - 1))

    gain = one(*split[0])
    for cut in split[1:]:
        gain = gain * one(*cut)
    return gain


def profile(count, total, limit, skew):
    weights = [(1 << 20) // math.isqrt(grade ** skew) + 1 for grade in range(2, count + 1)]
    surplus, holding = total - limit - (count - 1), [1] * (count - 1)
    while surplus > 0:
        candidates = [i for i in range(count - 1) if holding[i] < limit]
        whole, budget = sum([weights[i] for i in candidates]), surplus
        for i in candidates:
            addition = min(limit - holding[i], max(1, budget * weights[i] // whole), surplus)
            holding[i] = holding[i] + addition
            surplus = surplus - addition
    return np.array([limit] + holding)


def ragged_sizes(own_key, number_of, total, most, slope):
    if number_of == 2:
        one = jax.random.randint(own_key, (), max(1, total - most), min(most, total - 1) + 1)
        return jnp.stack([one, total - one])
    lengths = jnp.asarray(profile(number_of, total, most, slope), jnp.int32)
    couples = (number_of - 1) // 2
    donor, receiver = lengths[1:1 + 2 * couples:2], lengths[2:2 + 2 * couples:2]
    slack = jnp.minimum(donor - 1, most - receiver)
    moved = jax.random.randint(jax.random.fold_in(own_key, 1), (couples,), 0, 1 << 20) % (slack + 1)
    lengths = lengths.at[1:1 + 2 * couples:2].set(donor - moved).at[2:2 + 2 * couples:2].set(receiver + moved)
    return lengths[jax.random.permutation(jax.random.fold_in(own_key, 2), number_of)]


def bell_draw(key, extent, width, bound, cuts=(), kind=jnp.bfloat16):
    array = jax.random.normal(key, extent, jnp.float32) * width
    if len(cuts) > 0:
        array = block_scale(key, extent, cuts, -0.22, 0.18) * array
    return jnp.clip(array, min=-bound, max=bound).astype(kind)


def setup_inputs(seed: int = 0) -> dict:
    streams_of = jax.random.split(jax.random.key(seed), 8)
    return {
        "coefficients": bell_draw(streams_of[0], (K, M), 1.0, 6.0, ((0, 8), (1, 4))),
        "row_counts": ragged_sizes(streams_of[1], N_SUB, ROWS_MEAN * N_SUB, 2 * ROWS_MEAN, 2).astype(jnp.int32),
        "ancestors": draw_ancestors(jax.random.fold_in(streams_of[7], 71), 0),
        "interior_modes": bell_draw(streams_of[3], (N_SUB * PHYS, CAP), ROWS_MEAN ** -0.5, 0.25, ((0, 8),)),
        "separator_modes": bell_draw(streams_of[4], (N_SUB * BW, SEPM), SEPM ** -0.5, 0.5),
        "coupling": bell_draw(streams_of[5], (N_SUB * PHYS, LEVELS * BW), (LEVELS * BW // 2) ** -0.5, 0.3125, ((0, 8),)),
        "pattern": touch_ends((jax.random.randint(streams_of[6], (N_SUB, NBLK, LEVELS), 0, 2) < 1).astype(jnp.int32), jax.random.fold_in(streams_of[6], 1), 0, 1),
    }


def reference(coefficients, row_counts, ancestors, interior_modes, separator_modes, coupling, pattern):
    ordered = coefficients.reshape(N_SUB, N_VEC, K // (N_SUB * N_VEC), M)
    ordered = jnp.transpose(ordered, (1, 0, 2, 3)).reshape(K, M)
    offsets = (jnp.cumsum(row_counts) - row_counts).astype(jnp.int32)
    interior_total = ROWS_MEAN * N_SUB
    contract = (((1,), (1,)), ((), ()))

    def separator_one(index):
        start = (interior_total + index * SEPM).astype(jnp.int32)
        sep_coef = lax.dynamic_slice_in_dim(ordered, start, SEPM, 1)
        modes = lax.dynamic_slice_in_dim(separator_modes, (index * BW).astype(jnp.int32), BW, 0)
        return lax.dot_general(modes, sep_coef, contract, preferred_element_type=jnp.float32).astype(jnp.bfloat16)

    owners = jnp.arange(N_SUB, dtype=jnp.int32)
    separated = lax.map(separator_one, owners)

    def owner_one(index):
        positions = jnp.arange(CAP, dtype=jnp.int32)
        live = positions < row_counts[index]
        row_index = jnp.where(live, offsets[index] + positions, 0).astype(jnp.int32)
        picked = jnp.take(ordered, row_index, axis=1)
        picked = jnp.where(live[None, :], picked, jnp.zeros((), picked.dtype))
        modes = lax.dynamic_slice_in_dim(interior_modes, (index * PHYS).astype(jnp.int32), PHYS, 0)
        total = lax.dot_general(modes, picked, contract, preferred_element_type=jnp.float32)
        block = lax.dynamic_slice_in_dim(coupling, (index * PHYS).astype(jnp.int32), PHYS, 0)
        gates = pattern[index].astype(block.dtype)
        masked = (block.reshape(PHYS // BW, BW, LEVELS, BW) * gates[:, None, :, None]).reshape(PHYS, LEVELS * BW)
        above = jnp.take(separated, ancestors[index], axis=0).reshape(LEVELS * BW, K)
        total = total + jnp.dot(masked, above, preferred_element_type=jnp.float32)
        return total.astype(jnp.bfloat16)

    interior_field = lax.map(owner_one, owners).reshape(N_SUB * PHYS, K)
    separator_field = separated.reshape(N_SUB * BW, K)
    return interior_field, separator_field
```

```python
import functools

import jax
import jax.numpy as jnp
from jax import lax
from jax.experimental import pallas as pl
from jax.experimental.pallas import tpu as pltpu
from jax.sharding import PartitionSpec as P

BW = 256
SEPM = 128
LEVELS = 3
LANES = 128
ROWS = 16
CONTRACT = (((1,), (1,)), ((), ()))


def partner_pairs(count, turn):
    return [(i, i ^ turn) for i in range(count)]


def exchange(blocks, axis):
    count = len(blocks)
    sent = [lax.ppermute(blocks[k], axis, partner_pairs(count, k)) for k in range(1, count)]
    return [blocks[0]] + sent


def split_kernel(coef_ref, *refs):
    count = len(refs) - 1
    sems = refs[count]
    slice_cols = refs[0].shape[0]
    me = lax.axis_index("vec")
    copies = []
    for k in list(range(1, count)) + [0]:
        at = pl.multiple_of(jnp.bitwise_xor(me, k) * slice_cols, slice_cols)
        copy = pltpu.make_async_copy(coef_ref.at[pl.ds(at, slice_cols)], refs[k], sems.at[k])
        copy.start()
        copies.append(copy)
    for copy in copies:
        copy.wait()


def split(coefficients, count):
    shape = (coefficients.shape[0] // count, coefficients.shape[1])
    return pl.pallas_call(
        split_kernel,
        out_shape=[jax.ShapeDtypeStruct(shape, coefficients.dtype)] * count,
        in_specs=[pl.BlockSpec(memory_space=pl.ANY)],
        out_specs=[pl.BlockSpec(memory_space=pltpu.VMEM)] * count,
        scratch_shapes=[pltpu.SemaphoreType.DMA((count,))],
        compiler_params=pltpu.CompilerParams(vmem_limit_bytes=4 << 20),
        name="split_slices",
    )(coefficients)


def pack_kernel(interior_total, cap, sub_count, vec_count, direct, counts_ref, anc_ref, *refs):
    chunks, outs, rows_ref = refs[:vec_count], refs[vec_count : vec_count + sub_count], refs[-1]
    slice_cols, width = chunks[0].shape
    total = vec_count * width
    mine = lax.axis_index("vec") if direct else jnp.int32(0)
    sub = lax.axis_index("sub") if direct else jnp.int32(0)
    for k in range(vec_count):
        at = pl.multiple_of(jnp.bitwise_xor(mine, k) * width, LANES)
        rows_ref[:, pl.ds(at, width)] = chunks[k][...]
    if rows_ref.shape[1] > total:
        rows_ref[:, total:] = jnp.zeros((slice_cols, rows_ref.shape[1] - total), rows_ref.dtype)
    lane = lax.broadcasted_iota(jnp.int32, (slice_cols, LANES), 1)
    for k in range(sub_count):
        owner = jnp.bitwise_xor(sub, k)
        count = counts_ref[owner]
        offset = jnp.int32(0)
        for p in range(sub_count):
            offset = offset + jnp.where(p < owner, counts_ref[p], 0)
        start = offset // LANES
        shift = offset - start * LANES
        back = lax.rem(LANES - shift, LANES)
        base = pl.multiple_of(start * LANES, LANES)
        keep = lane < LANES - shift
        pieces = []
        for j in range(cap // LANES + 1):
            piece = rows_ref[:, pl.ds(base + j * LANES, LANES)].astype(jnp.float32)
            pieces.append(pltpu.roll(piece, back, 1))
        for j in range(cap // LANES):
            merged = jnp.where(keep, pieces[j], pieces[j + 1])
            merged = jnp.where(lane + j * LANES < count, merged, 0.0)
            outs[k][:, j * LANES : (j + 1) * LANES] = merged.astype(rows_ref.dtype)
        labels = [owner] + [anc_ref[l, owner] for l in range(LEVELS)]
        for n, label in enumerate(labels):
            at = pl.multiple_of(interior_total + label * SEPM, SEPM)
            outs[k][:, cap + n * SEPM : cap + (n + 1) * SEPM] = rows_ref[:, pl.ds(at, SEPM)]


def pack(chunks, row_counts, ancestors, cap, direct):
    vec_count = len(chunks)
    slice_cols, width = chunks[0].shape
    dtype = chunks[0].dtype
    sub_count = row_counts.shape[0]
    total = vec_count * width
    interior_total = total - sub_count * SEPM
    slot = cap + (LEVELS + 1) * SEPM
    smem, vmem = pl.BlockSpec(memory_space=pltpu.SMEM), pl.BlockSpec(memory_space=pltpu.VMEM)
    return pl.pallas_call(
        functools.partial(pack_kernel, interior_total, cap, sub_count, vec_count, direct),
        out_shape=[jax.ShapeDtypeStruct((slice_cols, slot), dtype)] * sub_count,
        in_specs=[smem, smem] + [vmem] * vec_count,
        out_specs=[vmem] * sub_count,
        scratch_shapes=[pltpu.VMEM((slice_cols, max(total, interior_total + cap)), dtype)],
        compiler_params=pltpu.CompilerParams(vmem_limit_bytes=8 << 20),
        name="pack_windows",
    )(row_counts, ancestors, *chunks)


def stage_kernel(
    anc_ref, pattern_ref, sep_ref, modes_ref, coupling_ref,
    sep_out, modes_out, coupling_out, sep_sem, modes_sem, coupling_sem,
):
    phys = coupling_out.shape[0]
    me = lax.axis_index("sub")
    whole = pltpu.make_async_copy(coupling_ref, coupling_out, coupling_sem)
    whole.start()
    parts = [pltpu.make_async_copy(modes_ref, modes_out, modes_sem)]
    for k in range(LEVELS + 1):
        label = me if k == 0 else anc_ref[k - 1, me]
        part = pltpu.make_async_copy(
            sep_ref.at[pl.ds(pl.multiple_of(label * BW, BW), BW)],
            sep_out.at[pl.ds(k * BW, BW)],
            sep_sem.at[k],
        )
        parts.append(part)
    for part in parts:
        part.start()
    whole.wait()
    for b in range(phys // BW):
        for l in range(LEVELS):

            @pl.when(pattern_ref[l, 0, b] == 0)
            def _(b=b, l=l):
                coupling_out[b * BW : (b + 1) * BW, l * BW : (l + 1) * BW] = jnp.zeros(
                    (BW, BW), coupling_out.dtype
                )

    for part in parts:
        part.wait()


def stage(ancestors, pattern, separator_modes, modes, coupling):
    hbm = pl.BlockSpec(memory_space=pl.ANY)
    smem, vmem = pl.BlockSpec(memory_space=pltpu.SMEM), pl.BlockSpec(memory_space=pltpu.VMEM)
    moved = 2 * separator_modes.size + 2 * coupling.size + 2 * modes.size
    return pl.pallas_call(
        stage_kernel,
        out_shape=(
            pltpu.VMEM(((LEVELS + 1) * BW, SEPM), coupling.dtype),
            pltpu.VMEM(modes.shape, modes.dtype),
            pltpu.VMEM(coupling.shape, coupling.dtype),
        ),
        in_specs=[smem, smem, hbm, hbm, hbm],
        out_specs=(vmem, vmem, vmem),
        scratch_shapes=[
            pltpu.SemaphoreType.DMA((LEVELS + 1,)),
            pltpu.SemaphoreType.DMA,
            pltpu.SemaphoreType.DMA,
        ],
        compiler_params=pltpu.CompilerParams(vmem_limit_bytes=4 << 20),
        cost_estimate=pl.CostEstimate(flops=0, transcendentals=0, bytes_accessed=moved),
        name="stage_operands",
    )(ancestors, pattern, separator_modes, modes, coupling)


def field_kernel(rows, slot_count, *refs):
    slots = refs[:slot_count]
    sep_ref, modes_ref, coupling_ref = refs[slot_count : slot_count + 3]
    field_ref, own_ref = refs[slot_count + 3 : slot_count + 5]
    got_ref, coef_ref, above_ref, block_ref, sems = refs[slot_count + 5 :]
    phys, cap = modes_ref.shape
    slice_cols = slots[0].shape[0]
    sub = lax.axis_index("sub")
    for k in range(slot_count):
        turned = jnp.bitwise_xor(sub, k) if slot_count > 1 else 0
        at = pl.multiple_of(turned * slice_cols, slice_cols)
        got_ref[pl.ds(at, slice_cols), :] = slots[k][...]
    coef_ref[...] = got_ref[:, :cap].T
    for k in range(LEVELS + 1):
        part = got_ref[:, cap + k * SEPM : cap + (k + 1) * SEPM]
        block = lax.dot_general(
            sep_ref[k * BW : (k + 1) * BW, :], part, CONTRACT, preferred_element_type=jnp.float32
        ).astype(jnp.bfloat16)
        if k == 0:
            own_ref[...] = block
        else:
            above_ref[(k - 1) * BW : k * BW, :] = block
    copies = []
    for s in range(phys // rows):
        at = slice(s * rows, (s + 1) * rows)
        acc = jnp.dot(modes_ref[at, :], coef_ref[...], preferred_element_type=jnp.float32)
        acc = acc + jnp.dot(coupling_ref[at, :], above_ref[...], preferred_element_type=jnp.float32)
        block_ref[at, :] = acc.astype(block_ref.dtype)
        copy = pltpu.make_async_copy(
            block_ref.at[pl.ds(s * rows, rows)], field_ref.at[pl.ds(s * rows, rows)], sems.at[s]
        )
        copy.start()
        copies.append(copy)
    for copy in copies:
        copy.wait()


def fields(slots, sep, modes, coupling):
    slot_count = len(slots)
    phys, cap = modes.shape
    group = slot_count * slots[0].shape[0]
    rows = 2 * BW
    vmem = pl.BlockSpec(memory_space=pltpu.VMEM)
    return pl.pallas_call(
        functools.partial(field_kernel, rows, slot_count),
        out_shape=(
            jax.ShapeDtypeStruct((phys, group), jnp.bfloat16),
            jax.ShapeDtypeStruct((BW, group), jnp.bfloat16),
        ),
        in_specs=[vmem] * (slot_count + 3),
        out_specs=(pl.BlockSpec(memory_space=pl.ANY), vmem),
        scratch_shapes=[
            pltpu.VMEM((group, slots[0].shape[1]), jnp.bfloat16),
            pltpu.VMEM((cap, group), jnp.bfloat16),
            pltpu.VMEM((LEVELS * BW, group), jnp.bfloat16),
            pltpu.VMEM((phys, group), jnp.bfloat16),
            pltpu.SemaphoreType.DMA((phys // rows,)),
        ],
        compiler_params=pltpu.CompilerParams(vmem_limit_bytes=16 << 20),
        name="interior_and_separator_fields",
    )(*slots, sep, modes, coupling)


def in_hbm(array):
    return pltpu.with_memory_space_constraint(array, pltpu.HBM)


def body(coefficients, row_counts, ancestors, interior_modes, separator_modes, coupling, pattern):
    vec_count, sub_count = lax.axis_size("vec"), lax.axis_size("sub")
    slice_cols = coefficients.shape[0] // vec_count
    cap = interior_modes.shape[1]
    counts = in_hbm(row_counts)
    above = in_hbm(ancestors.T)
    gates = in_hbm(jnp.transpose(pattern, (2, 0, 1)))
    powers = vec_count & (vec_count - 1) == 0 and sub_count & (sub_count - 1) == 0
    if powers and slice_cols % ROWS == 0:
        chunks = exchange(split(in_hbm(coefficients), vec_count), "vec")
        slots = exchange(pack(chunks, counts, above, cap, True), "sub")
    else:
        regrouped = coefficients.reshape(vec_count, slice_cols, coefficients.shape[1])
        regrouped = lax.all_to_all(regrouped, "vec", split_axis=0, concat_axis=0, tiled=True)
        slots = jnp.stack(pack(list(regrouped), counts, above, cap, False))
        slots = lax.all_to_all(slots, "sub", split_axis=0, concat_axis=0, tiled=True)
        slots = [slots.reshape(-1, slots.shape[2])]
    sep, modes, masked = stage(
        above, gates, in_hbm(separator_modes), in_hbm(interior_modes), in_hbm(coupling)
    )
    return fields(slots, sep, modes, masked)


def solution(mesh):
    placed = (P("sub", "vec"), P(), P(), P("sub", None), P(), P("sub", None), P("sub", None, None))
    return jax.shard_map(
        body,
        mesh=mesh,
        in_specs=placed,
        out_specs=(P("sub", "vec"), P("sub", "vec")),
        check_vma=False,
    )
```

```python
import functools

import jax
import jax.numpy as jnp
from jax import lax
from jax.experimental import pallas as pl
from jax.experimental.pallas import tpu as pltpu
from jax.sharding import PartitionSpec as P

BW = 256
SEPM = 128
LEVELS = 3
LANES = 128
ROWS = 16
ORD = [0, 1, 4, 2, 6, 5, 3, 7]
CUT = ()
CONTRACT = (((1,), (1,)), ((), ()))


def turn_over(block, axis, count, turn):
    return lax.ppermute(block, axis, [(i, i ^ turn) for i in range(count)])


def split_kernel(coef_ref, *refs):
    count = len(refs) - 1
    sems = refs[count]
    slice_cols = refs[0].shape[0]
    me = lax.axis_index("vec")
    copies = []
    for k in list(range(1, count)) + [0]:
        at = pl.multiple_of(jnp.bitwise_xor(me, k) * slice_cols, slice_cols)
        copy = pltpu.make_async_copy(coef_ref.at[pl.ds(at, slice_cols)], refs[k], sems.at[k])
        copy.start()
        copies.append(copy)
    for copy in copies:
        copy.wait()


def split(coefficients, count):
    shape = (coefficients.shape[0] // count, coefficients.shape[1])
    return pl.pallas_call(
        split_kernel,
        out_shape=[jax.ShapeDtypeStruct(shape, coefficients.dtype)] * count,
        in_specs=[pl.BlockSpec(memory_space=pl.ANY)],
        out_specs=[pl.BlockSpec(memory_space=pltpu.VMEM)] * count,
        scratch_shapes=[pltpu.SemaphoreType.DMA((count,))],
        compiler_params=pltpu.CompilerParams(vmem_limit_bytes=4 << 20),
        name="split_slices",
    )(coefficients)


def put_windows(rows_ref, out_ref, count, offset, cap, lane):
    start = offset // LANES
    shift = offset - start * LANES
    back = lax.rem(LANES - shift, LANES)
    base = pl.multiple_of(start * LANES, LANES)
    keep = lane < LANES - shift
    pieces = []
    for j in range(cap // LANES + 1):
        piece = rows_ref[:, pl.ds(base + j * LANES, LANES)].astype(jnp.float32)
        pieces.append(pltpu.roll(piece, back, 1))
    for j in range(cap // LANES):
        merged = jnp.where(keep, pieces[j], pieces[j + 1])
        merged = jnp.where(lane + j * LANES < count, merged, 0.0)
        out_ref[:, j * LANES : (j + 1) * LANES] = merged.astype(rows_ref.dtype)


def put_separators(from_ref, first, out_ref, to, owner, anc_ref):
    labels = [owner] + [anc_ref[l, owner] for l in range(LEVELS)]
    for n, label in enumerate(labels):
        at = pl.multiple_of(first + label * SEPM, SEPM)
        out_ref[:, to + n * SEPM : to + (n + 1) * SEPM] = from_ref[:, pl.ds(at, SEPM)]


def window_start(counts_ref, sub_count, owner):
    offset = jnp.int32(0)
    for p in range(sub_count):
        offset = offset + jnp.where(p < owner, counts_ref[p], 0)
    return offset


def pack_kernel(interior_total, cap, turns, direct, counts_ref, anc_ref, *refs):
    sub_count = counts_ref.shape[0]
    chunks, outs, rows_ref = refs[1 : -len(turns) - 1], refs[-len(turns) - 1 : -1], refs[-1]
    slice_cols, width = chunks[0].shape
    total = len(chunks) * width
    mine = lax.axis_index("vec") if direct else jnp.int32(0)
    sub = lax.axis_index("sub") if direct else jnp.int32(0)
    for k in range(len(chunks)):
        at = pl.multiple_of(jnp.bitwise_xor(mine, k) * width, LANES)
        rows_ref[:, pl.ds(at, width)] = chunks[k][...]
    if rows_ref.shape[1] > total:
        rows_ref[:, total:] = jnp.zeros((slice_cols, rows_ref.shape[1] - total), rows_ref.dtype)
    lane = lax.broadcasted_iota(jnp.int32, (slice_cols, LANES), 1)
    for out_ref, (turn, has_interior, has_separators) in zip(outs, turns):
        owner = jnp.bitwise_xor(sub, turn)
        if has_interior:
            offset = window_start(counts_ref, sub_count, owner)
            put_windows(rows_ref, out_ref, counts_ref[owner], offset, cap, lane)
        if has_separators:
            put_separators(rows_ref, interior_total, out_ref, cap * has_interior, owner, anc_ref)


def pack(token, chunks, row_counts, ancestors, cap, turns, direct):
    slice_cols, width = chunks[0].shape
    dtype = chunks[0].dtype
    sub_count = row_counts.shape[0]
    total = len(chunks) * width
    interior_total = total - sub_count * SEPM
    kept = (LEVELS + 1) * SEPM
    smem, vmem = pl.BlockSpec(memory_space=pltpu.SMEM), pl.BlockSpec(memory_space=pltpu.VMEM)
    return pl.pallas_call(
        functools.partial(pack_kernel, interior_total, cap, turns, direct),
        out_shape=[jax.ShapeDtypeStruct((slice_cols, cap * a + kept * b), dtype) for _, a, b in turns],
        in_specs=[smem, smem, pl.BlockSpec(memory_space=pl.ANY)] + [vmem] * len(chunks),
        out_specs=[vmem] * len(turns),
        scratch_shapes=[pltpu.VMEM((slice_cols, max(total, interior_total + cap)), dtype)],
        compiler_params=pltpu.CompilerParams(vmem_limit_bytes=8 << 20),
        name="pack_windows",
    )(row_counts, ancestors, token, *chunks)


def stage_modes_kernel(modes_ref, modes_out, token_ref, sem):
    whole = pltpu.make_async_copy(modes_ref, modes_out, sem)
    whole.start()
    token_ref[...] = jnp.zeros_like(token_ref)
    whole.wait()


def stage_modes(modes):
    vmem = pl.BlockSpec(memory_space=pltpu.VMEM)
    return pl.pallas_call(
        stage_modes_kernel,
        out_shape=(pltpu.VMEM(modes.shape, modes.dtype), pltpu.VMEM((8, LANES), jnp.float32)),
        in_specs=[pl.BlockSpec(memory_space=pl.ANY)],
        out_specs=(vmem, vmem),
        scratch_shapes=[pltpu.SemaphoreType.DMA],
        compiler_params=pltpu.CompilerParams(vmem_limit_bytes=4 << 20),
        cost_estimate=pl.CostEstimate(flops=0, transcendentals=0, bytes_accessed=2 * modes.size),
        name="stage_modes",
    )(modes)


def stage_kernel(
    anc_ref, pattern_ref, sep_ref, coupling_ref, sep_out, coupling_out, sep_sem, coupling_sem
):
    phys = coupling_out.shape[0]
    me = lax.axis_index("sub")
    whole = pltpu.make_async_copy(coupling_ref, coupling_out, coupling_sem)
    whole.start()
    parts = []
    for k in range(LEVELS + 1):
        label = me if k == 0 else anc_ref[k - 1, me]
        part = pltpu.make_async_copy(
            sep_ref.at[pl.ds(pl.multiple_of(label * BW, BW), BW)],
            sep_out.at[pl.ds(k * BW, BW)],
            sep_sem.at[k],
        )
        part.start()
        parts.append(part)
    whole.wait()
    for b in range(phys // BW):
        for l in range(LEVELS):

            @pl.when(pattern_ref[l, 0, b] == 0)
            def _(b=b, l=l):
                coupling_out[b * BW : (b + 1) * BW, l * BW : (l + 1) * BW] = jnp.zeros(
                    (BW, BW), coupling_out.dtype
                )

    for part in parts:
        part.wait()


def stage_coupling(ancestors, pattern, separator_modes, coupling):
    hbm = pl.BlockSpec(memory_space=pl.ANY)
    smem, vmem = pl.BlockSpec(memory_space=pltpu.SMEM), pl.BlockSpec(memory_space=pltpu.VMEM)
    return pl.pallas_call(
        stage_kernel,
        out_shape=(
            pltpu.VMEM(((LEVELS + 1) * BW, SEPM), coupling.dtype),
            pltpu.VMEM(coupling.shape, coupling.dtype),
        ),
        in_specs=[smem, smem, hbm, hbm],
        out_specs=(vmem, vmem),
        scratch_shapes=[pltpu.SemaphoreType.DMA((LEVELS + 1,)), pltpu.SemaphoreType.DMA],
        compiler_params=pltpu.CompilerParams(vmem_limit_bytes=4 << 20),
        cost_estimate=pl.CostEstimate(flops=0, transcendentals=0, bytes_accessed=2 * coupling.size),
        name="stage_coupling",
    )(ancestors, pattern, separator_modes, coupling)


def gather_rows(places, slots, got_ref):
    width = got_ref.shape[1]
    for n, lanes, turn in places:
        slice_cols = slots[n].shape[0]
        block = 0 if turn is None else jnp.bitwise_xor(lax.axis_index("sub"), turn)
        at = pl.multiple_of(block * slice_cols, slice_cols)
        got_ref[pl.ds(at, slice_cols), :] = slots[n][:, lanes : lanes + width]


def above_kernel(rows, places, slot_count, *refs):
    slots, (sep_ref, coupling_ref, total_ref, own_ref, got_ref, above_ref) = refs[:slot_count], refs[slot_count:]
    gather_rows(places, slots, got_ref)
    for k in range(LEVELS + 1):
        part = got_ref[:, k * SEPM : (k + 1) * SEPM]
        block = lax.dot_general(
            sep_ref[k * BW : (k + 1) * BW, :], part, CONTRACT, preferred_element_type=jnp.float32
        ).astype(jnp.bfloat16)
        if k == 0:
            own_ref[...] = block
        else:
            above_ref[(k - 1) * BW : k * BW, :] = block
    for s in range(coupling_ref.shape[0] // rows):
        at = slice(s * rows, (s + 1) * rows)
        total_ref[at, :] = jnp.dot(
            coupling_ref[at, :], above_ref[...], preferred_element_type=jnp.float32
        )


def above_fields(slots, places, group, sep, coupling):
    phys = coupling.shape[0]
    vmem = pl.BlockSpec(memory_space=pltpu.VMEM)
    return pl.pallas_call(
        functools.partial(above_kernel, 2 * BW, places, len(slots)),
        out_shape=(
            pltpu.VMEM((phys, group), jnp.float32),
            jax.ShapeDtypeStruct((BW, group), jnp.bfloat16),
        ),
        in_specs=[vmem] * (len(slots) + 2),
        out_specs=(vmem, vmem),
        scratch_shapes=[
            pltpu.VMEM((group, (LEVELS + 1) * SEPM), jnp.bfloat16),
            pltpu.VMEM((LEVELS * BW, group), jnp.bfloat16),
        ],
        compiler_params=pltpu.CompilerParams(vmem_limit_bytes=4 << 20),
        cost_estimate=pl.CostEstimate(
            flops=2 * coupling.size * group, transcendentals=0, bytes_accessed=2 * coupling.size
        ),
        name="separator_fields_and_coupling",
    )(*slots, sep, coupling)


def interior_kernel(rows, places, slot_count, *refs):
    slots, refs = refs[:slot_count], refs[slot_count:]
    modes_ref, total_ref, field_ref, got_ref, coef_ref, block_ref, sems = refs
    gather_rows(places, slots, got_ref)
    coef_ref[...] = got_ref[...].T
    copies = []
    for s in range(modes_ref.shape[0] // rows):
        at = slice(s * rows, (s + 1) * rows)
        acc = jnp.dot(modes_ref[at, :], coef_ref[...], preferred_element_type=jnp.float32)
        block_ref[at, :] = (acc + total_ref[at, :]).astype(block_ref.dtype)
        copy = pltpu.make_async_copy(
            block_ref.at[pl.ds(s * rows, rows)], field_ref.at[pl.ds(s * rows, rows)], sems.at[s]
        )
        copy.start()
        copies.append(copy)
    for copy in copies:
        copy.wait()


def interior(slots, places, group, modes, total):
    phys, cap = modes.shape
    rows = 2 * BW
    vmem = pl.BlockSpec(memory_space=pltpu.VMEM)
    return pl.pallas_call(
        functools.partial(interior_kernel, rows, places, len(slots)),
        out_shape=jax.ShapeDtypeStruct((phys, group), jnp.bfloat16),
        in_specs=[vmem] * (len(slots) + 2),
        out_specs=pl.BlockSpec(memory_space=pl.ANY),
        scratch_shapes=[
            pltpu.VMEM((group, cap), jnp.bfloat16),
            pltpu.VMEM((cap, group), jnp.bfloat16),
            pltpu.VMEM((phys, group), jnp.bfloat16),
            pltpu.SemaphoreType.DMA((phys // rows,)),
        ],
        compiler_params=pltpu.CompilerParams(vmem_limit_bytes=8 << 20),
        name="interior_field",
    )(*slots, modes, total)


def in_hbm(array):
    return pltpu.with_memory_space_constraint(array, pltpu.HBM)


def turn_order(count):
    half = count // 2
    first = [k for k in range(half)]
    return ORD if count == 8 else first + list(range(half, count))


def body(coefficients, row_counts, ancestors, interior_modes, separator_modes, coupling, pattern):
    vec_count, sub_count = lax.axis_size("vec"), lax.axis_size("sub")
    slice_cols = coefficients.shape[0] // vec_count
    group = slice_cols * sub_count
    cap = interior_modes.shape[1]
    kept = (LEVELS + 1) * SEPM
    counts = in_hbm(row_counts)
    above = in_hbm(ancestors.T)
    gates = in_hbm(jnp.transpose(pattern, (2, 0, 1)))
    modes, token = stage_modes(in_hbm(interior_modes))
    sep, masked = stage_coupling(above, gates, in_hbm(separator_modes), in_hbm(coupling))
    powers = vec_count & (vec_count - 1) == 0 and sub_count & (sub_count - 1) == 0
    if powers and sub_count > 1 and slice_cols % ROWS == 0:
        blocks = split(in_hbm(coefficients), vec_count)
        chunks = [turn_over(blocks[k], "vec", vec_count, k) if k else blocks[0] for k in range(vec_count)]
        turns = []
        for k in turn_order(sub_count):
            turns += [(k, 0, 1), (k, 1, 0)] if k in CUT else [(k, 1, 1)]
        packed = pack(token, chunks, counts, above, cap, turns, True)
        slots = [turn_over(p, "sub", sub_count, t[0]) if t[0] else p for p, t in zip(packed, turns)]
        early = [n for n in range(len(turns)) if turns[n][2]]
        late = [n for n in range(len(turns)) if turns[n][1]]
        above_places = [(i, cap * turns[n][1], turns[n][0]) for i, n in enumerate(early)]
        places = [(i, 0, turns[n][0]) for i, n in enumerate(late)]
        early, late = [slots[n] for n in early], [slots[n] for n in late]
    else:
        regrouped = coefficients.reshape(vec_count, slice_cols, coefficients.shape[1])
        regrouped = lax.all_to_all(regrouped, "vec", split_axis=0, concat_axis=0, tiled=True)
        turns = [(k, 1, 1) for k in range(sub_count)]
        slots = pack(token, list(regrouped), counts, above, cap, turns, False)
        slots = lax.all_to_all(jnp.stack(slots), "sub", split_axis=0, concat_axis=0, tiled=True)
        early = late = [slots.reshape(group, cap + kept)]
        above_places, places = [(0, cap, None)], [(0, 0, None)]
    total, own = above_fields(early, above_places, group, sep, masked)
    return interior(late, places, group, modes, total), own


def solution(mesh):
    placed = (P("sub", "vec"), P(), P(), P("sub", None), P(), P("sub", None), P("sub", None, None))
    return jax.shard_map(
        body,
        mesh=mesh,
        in_specs=placed,
        out_specs=(P("sub", "vec"), P("sub", "vec")),
        check_vma=False,
    )
```

```python
import functools

import jax
import jax.numpy as jnp
from jax import lax
from jax.experimental import pallas as pl
from jax.experimental.pallas import tpu as pltpu
from jax.sharding import PartitionSpec as P

BW = 256
SEPM = 128
LEVELS = 3
LANES = 128
ROWS = 16
EARLY_ORDER = [0, 4, 6, 1, 5, 3, 2, 7]
CUT = (4, 6)
LATE_ORDER = [0, 4, 6, 5, 1, 3, 2, 7]
VEC_ORDER = [2, 3, 1, 0]
AHEAD = 6 << 30
CONTRACT = (((1,), (1,)), ((), ()))


def turn_over(block, axis, count, turn):
    return lax.ppermute(block, axis, [(i, i ^ turn) for i in range(count)])


def split_kernel(coef_ref, *refs):
    count = len(refs) - 1
    sems = refs[count]
    slice_cols = refs[0].shape[0]
    me = lax.axis_index("vec")
    copies = []
    for k in list(range(1, count)) + [0]:
        at = pl.multiple_of(jnp.bitwise_xor(me, k) * slice_cols, slice_cols)
        copy = pltpu.make_async_copy(coef_ref.at[pl.ds(at, slice_cols)], refs[k], sems.at[k])
        copy.start()
        copies.append(copy)
    for copy in copies:
        copy.wait()


def split(coefficients, count):
    shape = (coefficients.shape[0] // count, coefficients.shape[1])
    return pl.pallas_call(
        split_kernel,
        out_shape=[jax.ShapeDtypeStruct(shape, coefficients.dtype)] * count,
        in_specs=[pl.BlockSpec(memory_space=pl.ANY)],
        out_specs=[pl.BlockSpec(memory_space=pltpu.VMEM)] * count,
        scratch_shapes=[pltpu.SemaphoreType.DMA((count,))],
        compiler_params=pltpu.CompilerParams(vmem_limit_bytes=4 << 20),
        cost_estimate=pl.CostEstimate(flops=AHEAD, transcendentals=0, bytes_accessed=1 << 20),
        name="split_slices",
    )(coefficients)


def put_windows(rows_ref, out_ref, count, offset, cap, lane):
    start = offset // LANES
    shift = offset - start * LANES
    back = lax.rem(LANES - shift, LANES)
    base = pl.multiple_of(start * LANES, LANES)
    keep = lane < LANES - shift
    pieces = []
    for j in range(cap // LANES + 1):
        piece = rows_ref[:, pl.ds(base + j * LANES, LANES)].astype(jnp.float32)
        pieces.append(pltpu.roll(piece, back, 1))
    for j in range(cap // LANES):
        merged = jnp.where(keep, pieces[j], pieces[j + 1])
        merged = jnp.where(lane + j * LANES < count, merged, 0.0)
        out_ref[:, j * LANES : (j + 1) * LANES] = merged.astype(rows_ref.dtype)


def put_separators(from_ref, first, out_ref, to, owner, anc_ref):
    labels = [owner] + [anc_ref[l, owner] for l in range(LEVELS)]
    for n, label in enumerate(labels):
        at = pl.multiple_of(first + label * SEPM, SEPM)
        out_ref[:, to + n * SEPM : to + (n + 1) * SEPM] = from_ref[:, pl.ds(at, SEPM)]


def window_start(counts_ref, sub_count, owner):
    offset = jnp.int32(0)
    for p in range(sub_count):
        offset = offset + jnp.where(p < owner, counts_ref[p], 0)
    return offset


def pack_kernel(interior_total, cap, turns, direct, chunk_turns, counts_ref, anc_ref, *refs):
    sub_count = counts_ref.shape[0]
    chunks, outs, rows_ref = refs[1 : -len(turns) - 1], refs[-len(turns) - 1 : -1], refs[-1]
    slice_cols, width = chunks[0].shape
    total = len(chunks) * width
    mine = lax.axis_index("vec") if direct else jnp.int32(0)
    sub = lax.axis_index("sub") if direct else jnp.int32(0)
    for chunk, turn in zip(chunks, chunk_turns):
        at = pl.multiple_of(jnp.bitwise_xor(mine, turn) * width, LANES)
        rows_ref[:, pl.ds(at, width)] = chunk[...]
    if rows_ref.shape[1] > total:
        rows_ref[:, total:] = jnp.zeros((slice_cols, rows_ref.shape[1] - total), rows_ref.dtype)
    lane = lax.broadcasted_iota(jnp.int32, (slice_cols, LANES), 1)
    for out_ref, (turn, has_interior, has_separators) in zip(outs, turns):
        owner = jnp.bitwise_xor(sub, turn)
        if has_interior:
            offset = window_start(counts_ref, sub_count, owner)
            put_windows(rows_ref, out_ref, counts_ref[owner], offset, cap, lane)
        if has_separators:
            put_separators(rows_ref, interior_total, out_ref, cap * has_interior, owner, anc_ref)


def pack(token, chunks, chunk_turns, row_counts, ancestors, cap, turns, direct):
    slice_cols, width = chunks[0].shape
    dtype = chunks[0].dtype
    sub_count = row_counts.shape[0]
    total = len(chunks) * width
    interior_total = total - sub_count * SEPM
    kept = (LEVELS + 1) * SEPM
    smem, vmem = pl.BlockSpec(memory_space=pltpu.SMEM), pl.BlockSpec(memory_space=pltpu.VMEM)
    return pl.pallas_call(
        functools.partial(pack_kernel, interior_total, cap, turns, direct, chunk_turns),
        out_shape=[jax.ShapeDtypeStruct((slice_cols, cap * a + kept * b), dtype) for _, a, b in turns],
        in_specs=[smem, smem, pl.BlockSpec(memory_space=pl.ANY)] + [vmem] * len(chunks),
        out_specs=[vmem] * len(turns),
        scratch_shapes=[pltpu.VMEM((slice_cols, max(total, interior_total + cap)), dtype)],
        compiler_params=pltpu.CompilerParams(vmem_limit_bytes=8 << 20),
        name="pack_windows",
    )(row_counts, ancestors, token, *chunks)


def mask_kernel(anc_ref, pattern_ref, sep_ref, coupling_ref, sep_out, coupling_out):
    me = lax.axis_index("sub")
    for k in range(LEVELS + 1):
        label = me if k == 0 else anc_ref[k - 1, me]
        at = pl.multiple_of(label * BW, BW)
        sep_out[k * BW : (k + 1) * BW, :] = sep_ref[pl.ds(at, BW), :]
    for b in range(coupling_ref.shape[0] // BW):
        for l in range(LEVELS):
            live = pattern_ref[l, 0, b] != 0
            at = (slice(b * BW, (b + 1) * BW), slice(l * BW, (l + 1) * BW))
            part = coupling_ref[at]
            coupling_out[at] = jnp.where(live, part, jnp.zeros_like(part))


def mask(ancestors, pattern, separator_modes, coupling):
    smem, vmem = pl.BlockSpec(memory_space=pltpu.SMEM), pl.BlockSpec(memory_space=pltpu.VMEM)
    return pl.pallas_call(
        mask_kernel,
        out_shape=(
            pltpu.VMEM(((LEVELS + 1) * BW, SEPM), coupling.dtype),
            pltpu.VMEM(coupling.shape, coupling.dtype),
        ),
        in_specs=[smem, smem, vmem, vmem],
        out_specs=(vmem, vmem),
        compiler_params=pltpu.CompilerParams(vmem_limit_bytes=4 << 20),
        cost_estimate=pl.CostEstimate(flops=0, transcendentals=0, bytes_accessed=2 * coupling.size),
        name="mask_coupling",
    )(ancestors, pattern, separator_modes, coupling)


def gather_rows(places, slots, got_ref):
    width = got_ref.shape[1]
    for n, lanes, turn in places:
        slice_cols = slots[n].shape[0]
        block = 0 if turn is None else jnp.bitwise_xor(lax.axis_index("sub"), turn)
        at = pl.multiple_of(block * slice_cols, slice_cols)
        got_ref[pl.ds(at, slice_cols), :] = slots[n][:, lanes : lanes + width]


def above_kernel(rows, places, slot_count, *refs):
    slots, (sep_ref, coupling_ref, total_ref, own_ref, got_ref, above_ref) = refs[:slot_count], refs[slot_count:]
    gather_rows(places, slots, got_ref)
    for k in range(LEVELS + 1):
        part = got_ref[:, k * SEPM : (k + 1) * SEPM]
        block = lax.dot_general(
            sep_ref[k * BW : (k + 1) * BW, :], part, CONTRACT, preferred_element_type=jnp.float32
        ).astype(jnp.bfloat16)
        if k == 0:
            own_ref[...] = block
        else:
            above_ref[(k - 1) * BW : k * BW, :] = block
    for s in range(coupling_ref.shape[0] // rows):
        at = slice(s * rows, (s + 1) * rows)
        total_ref[at, :] = jnp.dot(
            coupling_ref[at, :], above_ref[...], preferred_element_type=jnp.float32
        )


def above_fields(slots, places, group, sep, coupling):
    phys = coupling.shape[0]
    vmem = pl.BlockSpec(memory_space=pltpu.VMEM)
    return pl.pallas_call(
        functools.partial(above_kernel, 2 * BW, places, len(slots)),
        out_shape=(
            pltpu.VMEM((phys, group), jnp.float32),
            jax.ShapeDtypeStruct((BW, group), jnp.bfloat16),
        ),
        in_specs=[vmem] * (len(slots) + 2),
        out_specs=(vmem, vmem),
        scratch_shapes=[
            pltpu.VMEM((group, (LEVELS + 1) * SEPM), jnp.bfloat16),
            pltpu.VMEM((LEVELS * BW, group), jnp.bfloat16),
        ],
        compiler_params=pltpu.CompilerParams(vmem_limit_bytes=4 << 20),
        cost_estimate=pl.CostEstimate(
            flops=2 * coupling.size * group, transcendentals=0, bytes_accessed=2 * coupling.size
        ),
        name="separator_fields_and_coupling",
    )(*slots, sep, coupling)


def interior_kernel(rows, places, slot_count, *refs):
    slots, refs = refs[:slot_count], refs[slot_count:]
    modes_ref, total_ref, field_ref, got_ref, coef_ref, block_ref, sems = refs
    gather_rows(places, slots, got_ref)
    coef_ref[...] = got_ref[...].T
    copies = []
    for s in range(modes_ref.shape[0] // rows):
        at = slice(s * rows, (s + 1) * rows)
        acc = jnp.dot(modes_ref[at, :], coef_ref[...], preferred_element_type=jnp.float32)
        block_ref[at, :] = (acc + total_ref[at, :]).astype(block_ref.dtype)
        copy = pltpu.make_async_copy(
            block_ref.at[pl.ds(s * rows, rows)], field_ref.at[pl.ds(s * rows, rows)], sems.at[s]
        )
        copy.start()
        copies.append(copy)
    for copy in copies:
        copy.wait()


def interior(slots, places, group, modes, total):
    phys, cap = modes.shape
    rows = 2 * BW
    vmem = pl.BlockSpec(memory_space=pltpu.VMEM)
    return pl.pallas_call(
        functools.partial(interior_kernel, rows, places, len(slots)),
        out_shape=jax.ShapeDtypeStruct((phys, group), jnp.bfloat16),
        in_specs=[vmem] * (len(slots) + 2),
        out_specs=pl.BlockSpec(memory_space=pl.ANY),
        scratch_shapes=[
            pltpu.VMEM((group, cap), jnp.bfloat16),
            pltpu.VMEM((cap, group), jnp.bfloat16),
            pltpu.VMEM((phys, group), jnp.bfloat16),
            pltpu.SemaphoreType.DMA((phys // rows,)),
        ],
        compiler_params=pltpu.CompilerParams(vmem_limit_bytes=8 << 20),
        name="interior_field",
    )(*slots, modes, total)


def in_hbm(array):
    return pltpu.with_memory_space_constraint(array, pltpu.HBM)


def turn_order(count, order):
    return order if count == len(order) else list(range(count))


def body(coefficients, row_counts, ancestors, interior_modes, separator_modes, coupling, pattern):
    vec_count, sub_count = lax.axis_size("vec"), lax.axis_size("sub")
    slice_cols = coefficients.shape[0] // vec_count
    group = slice_cols * sub_count
    cap = interior_modes.shape[1]
    kept = (LEVELS + 1) * SEPM
    counts = in_hbm(row_counts)
    above = in_hbm(ancestors.T)
    gates = in_hbm(jnp.transpose(pattern, (2, 0, 1)))
    sep, masked = mask(above, gates, separator_modes, coupling)
    powers = vec_count & (vec_count - 1) == 0 and sub_count & (sub_count - 1) == 0
    if powers and sub_count > 1 and slice_cols % ROWS == 0:
        blocks = split(in_hbm(coefficients), vec_count)
        chunk_turns = turn_order(vec_count, VEC_ORDER)
        chunks = [turn_over(blocks[k], "vec", vec_count, k) if k else blocks[0] for k in chunk_turns]
        turns = []
        for k in turn_order(sub_count, EARLY_ORDER):
            turns += [(k, 0, 1), (k, 1, 0)] if k in CUT else [(k, 1, 1)]
        packed = pack(sep, chunks, chunk_turns, counts, above, cap, turns, True)
        slots = [turn_over(p, "sub", sub_count, t[0]) if t[0] else p for p, t in zip(packed, turns)]
        early = [n for n in range(len(turns)) if turns[n][2]]
        late = [n for n in range(len(turns)) if turns[n][1]]
        late.sort(key=lambda n: turn_order(sub_count, LATE_ORDER).index(turns[n][0]))
        above_places = [(i, cap * turns[n][1], turns[n][0]) for i, n in enumerate(early)]
        places = [(i, 0, turns[n][0]) for i, n in enumerate(late)]
        early, late = [slots[n] for n in early], [slots[n] for n in late]
    else:
        regrouped = coefficients.reshape(vec_count, slice_cols, coefficients.shape[1])
        regrouped = lax.all_to_all(regrouped, "vec", split_axis=0, concat_axis=0, tiled=True)
        turns = [(k, 1, 1) for k in range(sub_count)]
        slots = pack(sep, list(regrouped), list(range(vec_count)), counts, above, cap, turns, False)
        slots = lax.all_to_all(jnp.stack(slots), "sub", split_axis=0, concat_axis=0, tiled=True)
        early = late = [slots.reshape(group, cap + kept)]
        above_places, places = [(0, cap, None)], [(0, 0, None)]
    total, own = above_fields(early, above_places, group, sep, masked)
    return interior(late, places, group, interior_modes, total), own


def solution(mesh):
    placed = (P("sub", "vec"), P(), P(), P("sub", None), P(), P("sub", None), P("sub", None, None))
    return jax.shard_map(
        body,
        mesh=mesh,
        in_specs=placed,
        out_specs=(P("sub", "vec"), P("sub", "vec")),
        check_vma=False,
    )
```

```python
import functools

import jax
import jax.numpy as jnp
from jax import lax
from jax.experimental import pallas as pl
from jax.experimental.pallas import tpu as pltpu
from jax.sharding import PartitionSpec as P

BW = 256
SEPM = 128
LEVELS = 3
LANES = 128
ROWS = 16
EARLY_ORDER = [0, 4, 6, 1, 5, 3, 2, 7]
CUT = (4, 6)
LATE_ORDER = [0, 4, 6, 5, 1, 3, 2, 7]
PART = 0
VEC_ORDER = [2, 1, 3, 0]
AHEAD = 6 << 30
CONTRACT = (((1,), (1,)), ((), ()))


def turn_over(block, axis, count, turn):
    return lax.ppermute(block, axis, [(i, i ^ turn) for i in range(count)])


def split_kernel(coef_ref, *refs):
    count = len(refs) - 1
    sems = refs[count]
    slice_cols = refs[0].shape[0]
    me = lax.axis_index("vec")
    copies = []
    for k in list(range(1, count)) + [0]:
        at = pl.multiple_of(jnp.bitwise_xor(me, k) * slice_cols, slice_cols)
        copy = pltpu.make_async_copy(coef_ref.at[pl.ds(at, slice_cols)], refs[k], sems.at[k])
        copy.start()
        copies.append(copy)
    for copy in copies:
        copy.wait()


def split(coefficients, count):
    shape = (coefficients.shape[0] // count, coefficients.shape[1])
    return pl.pallas_call(
        split_kernel,
        out_shape=[jax.ShapeDtypeStruct(shape, coefficients.dtype)] * count,
        in_specs=[pl.BlockSpec(memory_space=pl.ANY)],
        out_specs=[pl.BlockSpec(memory_space=pltpu.VMEM)] * count,
        scratch_shapes=[pltpu.SemaphoreType.DMA((count,))],
        compiler_params=pltpu.CompilerParams(vmem_limit_bytes=4 << 20),
        cost_estimate=pl.CostEstimate(flops=AHEAD, transcendentals=0, bytes_accessed=1 << 20),
        name="split_slices",
    )(coefficients)


def put_windows(rows_ref, out_ref, count, offset, first, last, lane):
    start = offset // LANES
    shift = offset - start * LANES
    back = lax.rem(LANES - shift, LANES)
    base = pl.multiple_of(start * LANES, LANES)
    keep = lane < LANES - shift
    pieces = {}
    for j in range(first // LANES, last // LANES + 1):
        piece = rows_ref[:, pl.ds(base + j * LANES, LANES)].astype(jnp.float32)
        pieces[j] = pltpu.roll(piece, back, 1)
    for j in range(first // LANES, last // LANES):
        merged = jnp.where(keep, pieces[j], pieces[j + 1])
        merged = jnp.where(lane + j * LANES < count, merged, 0.0)
        at = j * LANES - first
        out_ref[:, at : at + LANES] = merged.astype(rows_ref.dtype)


def put_separators(from_ref, first, out_ref, to, owner, anc_ref):
    labels = [owner] + [anc_ref[l, owner] for l in range(LEVELS)]
    for n, label in enumerate(labels):
        at = pl.multiple_of(first + label * SEPM, SEPM)
        out_ref[:, to + n * SEPM : to + (n + 1) * SEPM] = from_ref[:, pl.ds(at, SEPM)]


def window_start(counts_ref, sub_count, owner):
    offset = jnp.int32(0)
    for p in range(sub_count):
        offset = offset + jnp.where(p < owner, counts_ref[p], 0)
    return offset


def pack_kernel(interior_total, cap, turns, direct, chunk_turns, counts_ref, anc_ref, *refs):
    sub_count = counts_ref.shape[0]
    chunks, outs, rows_ref = refs[1 : -len(turns) - 1], refs[-len(turns) - 1 : -1], refs[-1]
    slice_cols, width = chunks[0].shape
    total = len(chunks) * width
    mine = lax.axis_index("vec") if direct else jnp.int32(0)
    sub = lax.axis_index("sub") if direct else jnp.int32(0)
    for chunk, turn in zip(chunks, chunk_turns):
        at = pl.multiple_of(jnp.bitwise_xor(mine, turn) * width, LANES)
        rows_ref[:, pl.ds(at, width)] = chunk[...]
    if rows_ref.shape[1] > total:
        rows_ref[:, total:] = jnp.zeros((slice_cols, rows_ref.shape[1] - total), rows_ref.dtype)
    lane = lax.broadcasted_iota(jnp.int32, (slice_cols, LANES), 1)
    for out_ref, (turn, first, last, has_separators) in zip(outs, turns):
        owner = jnp.bitwise_xor(sub, turn)
        if last > first:
            offset = window_start(counts_ref, sub_count, owner)
            put_windows(rows_ref, out_ref, counts_ref[owner], offset, first, last, lane)
        if has_separators:
            put_separators(rows_ref, interior_total, out_ref, last - first, owner, anc_ref)


def pack(token, chunks, chunk_turns, row_counts, ancestors, cap, turns, direct):
    slice_cols, width = chunks[0].shape
    dtype = chunks[0].dtype
    sub_count = row_counts.shape[0]
    total = len(chunks) * width
    interior_total = total - sub_count * SEPM
    kept = (LEVELS + 1) * SEPM
    smem, vmem = pl.BlockSpec(memory_space=pltpu.SMEM), pl.BlockSpec(memory_space=pltpu.VMEM)
    return pl.pallas_call(
        functools.partial(pack_kernel, interior_total, cap, turns, direct, chunk_turns),
        out_shape=[jax.ShapeDtypeStruct((slice_cols, b - a + kept * c), dtype) for _, a, b, c in turns],
        in_specs=[smem, smem, pl.BlockSpec(memory_space=pl.ANY)] + [vmem] * len(chunks),
        out_specs=[vmem] * len(turns),
        scratch_shapes=[pltpu.VMEM((slice_cols, max(total, interior_total + cap)), dtype)],
        compiler_params=pltpu.CompilerParams(vmem_limit_bytes=8 << 20),
        name="pack_windows",
    )(row_counts, ancestors, token, *chunks)


def mask_kernel(
    counts_ref, anc_ref, pattern_ref, sep_ref, coupling_ref, sep_out, coupling_out, count_out
):
    me = lax.axis_index("sub")
    count_out[...] = jnp.full(count_out.shape, counts_ref[me], jnp.int32)
    for k in range(LEVELS + 1):
        label = me if k == 0 else anc_ref[k - 1, me]
        at = pl.multiple_of(label * BW, BW)
        sep_out[k * BW : (k + 1) * BW, :] = sep_ref[pl.ds(at, BW), :]
    for b in range(coupling_ref.shape[0] // BW):
        for l in range(LEVELS):
            live = pattern_ref[l, 0, b] != 0
            at = (slice(b * BW, (b + 1) * BW), slice(l * BW, (l + 1) * BW))
            part = coupling_ref[at]
            coupling_out[at] = jnp.where(live, part, jnp.zeros_like(part))


def mask(row_counts, ancestors, pattern, separator_modes, coupling):
    smem, vmem = pl.BlockSpec(memory_space=pltpu.SMEM), pl.BlockSpec(memory_space=pltpu.VMEM)
    return pl.pallas_call(
        mask_kernel,
        out_shape=(
            pltpu.VMEM(((LEVELS + 1) * BW, SEPM), coupling.dtype),
            pltpu.VMEM(coupling.shape, coupling.dtype),
            pltpu.VMEM((8, LANES), jnp.int32),
        ),
        in_specs=[smem, smem, smem, vmem, vmem],
        out_specs=(vmem, vmem, vmem),
        compiler_params=pltpu.CompilerParams(vmem_limit_bytes=4 << 20),
        cost_estimate=pl.CostEstimate(flops=0, transcendentals=0, bytes_accessed=2 * coupling.size),
        name="mask_coupling",
    )(row_counts, ancestors, pattern, separator_modes, coupling)


def gather_rows(places, slots, got_ref):
    for n, lanes, first, last, turn in places:
        slice_cols = slots[n].shape[0]
        block = 0 if turn is None else jnp.bitwise_xor(lax.axis_index("sub"), turn)
        at = pl.multiple_of(block * slice_cols, slice_cols)
        got_ref[pl.ds(at, slice_cols), first:last] = slots[n][:, lanes : lanes + last - first]


def above_kernel(rows, places, slot_count, *refs):
    slots, (sep_ref, coupling_ref, total_ref, own_ref, got_ref, above_ref) = refs[:slot_count], refs[slot_count:]
    gather_rows(places, slots, got_ref)
    for k in range(LEVELS + 1):
        part = got_ref[:, k * SEPM : (k + 1) * SEPM]
        block = lax.dot_general(
            sep_ref[k * BW : (k + 1) * BW, :], part, CONTRACT, preferred_element_type=jnp.float32
        ).astype(jnp.bfloat16)
        if k == 0:
            own_ref[...] = block
        else:
            above_ref[(k - 1) * BW : k * BW, :] = block
    for s in range(coupling_ref.shape[0] // rows):
        at = slice(s * rows, (s + 1) * rows)
        total_ref[at, :] = jnp.dot(
            coupling_ref[at, :], above_ref[...], preferred_element_type=jnp.float32
        )


def above_fields(slots, places, group, sep, coupling):
    phys = coupling.shape[0]
    vmem = pl.BlockSpec(memory_space=pltpu.VMEM)
    return pl.pallas_call(
        functools.partial(above_kernel, 2 * BW, places, len(slots)),
        out_shape=(
            pltpu.VMEM((phys, group), jnp.float32),
            jax.ShapeDtypeStruct((BW, group), jnp.bfloat16),
        ),
        in_specs=[vmem] * (len(slots) + 2),
        out_specs=(vmem, vmem),
        scratch_shapes=[
            pltpu.VMEM((group, (LEVELS + 1) * SEPM), jnp.bfloat16),
            pltpu.VMEM((LEVELS * BW, group), jnp.bfloat16),
        ],
        compiler_params=pltpu.CompilerParams(vmem_limit_bytes=4 << 20),
        cost_estimate=pl.CostEstimate(
            flops=2 * coupling.size * group, transcendentals=0, bytes_accessed=2 * coupling.size
        ),
        name="separator_fields_and_coupling",
    )(*slots, sep, coupling)


def interior_kernel(rows, places, slot_count, *refs):
    slots, refs = refs[:slot_count], refs[slot_count:]
    count_ref, modes_ref, total_ref, field_ref, got_ref, coef_ref, block_ref, sems = refs
    phys, cap = modes_ref.shape
    tiles = (jnp.max(count_ref[...]) + BW - 1) // BW
    gather_rows(places, slots, got_ref)
    copies = [
        pltpu.make_async_copy(block_ref.at[pl.ds(at, rows)], field_ref.at[pl.ds(at, rows)], sems.at[n])
        for n, at in enumerate(range(0, phys, rows))
    ]
    for used in range(1, cap // BW + 1):

        @pl.when(tiles == used)
        def _(depth=used * BW):
            coef_ref[:depth, :] = got_ref[:, :depth].T
            for n, first in enumerate(range(0, phys, rows)):
                at = slice(first, first + rows)
                acc = jnp.dot(
                    modes_ref[at, :depth], coef_ref[:depth, :], preferred_element_type=jnp.float32
                )
                block_ref[at, :] = (acc + total_ref[at, :]).astype(block_ref.dtype)
                copies[n].start()

    for copy in copies:
        copy.wait()


def interior(slots, places, group, count, modes, total):
    phys, cap = modes.shape
    rows = 2 * BW
    vmem = pl.BlockSpec(memory_space=pltpu.VMEM)
    return pl.pallas_call(
        functools.partial(interior_kernel, rows, places, len(slots)),
        out_shape=jax.ShapeDtypeStruct((phys, group), jnp.bfloat16),
        in_specs=[vmem] * (len(slots) + 3),
        out_specs=pl.BlockSpec(memory_space=pl.ANY),
        scratch_shapes=[
            pltpu.VMEM((group, cap), jnp.bfloat16),
            pltpu.VMEM((cap, group), jnp.bfloat16),
            pltpu.VMEM((phys, group), jnp.bfloat16),
            pltpu.SemaphoreType.DMA((phys // rows,)),
        ],
        compiler_params=pltpu.CompilerParams(vmem_limit_bytes=8 << 20),
        name="interior_field",
    )(*slots, count, modes, total)


def in_hbm(array):
    return pltpu.with_memory_space_constraint(array, pltpu.HBM)


def turn_order(count, order):
    return order if count == len(order) else list(range(count))


def body(coefficients, row_counts, ancestors, interior_modes, separator_modes, coupling, pattern):
    vec_count, sub_count = lax.axis_size("vec"), lax.axis_size("sub")
    slice_cols = coefficients.shape[0] // vec_count
    group = slice_cols * sub_count
    cap = interior_modes.shape[1]
    kept = (LEVELS + 1) * SEPM
    counts = in_hbm(row_counts)
    above = in_hbm(ancestors.T)
    gates = in_hbm(jnp.transpose(pattern, (2, 0, 1)))
    sep, masked, count = mask(counts, above, gates, separator_modes, coupling)
    powers = vec_count & (vec_count - 1) == 0 and sub_count & (sub_count - 1) == 0
    if powers and sub_count > 1 and slice_cols % ROWS == 0:
        blocks = split(in_hbm(coefficients), vec_count)
        chunk_turns = turn_order(vec_count, VEC_ORDER)
        chunks = [turn_over(blocks[k], "vec", vec_count, k) if k else blocks[0] for k in chunk_turns]
        turns = []
        for k in turn_order(sub_count, EARLY_ORDER):
            part = min(PART, cap)
            turns += [(k, 0, part, 1), (k, part, cap, 0)] if k in CUT else [(k, 0, cap, 1)]
        packed = pack(sep, chunks, chunk_turns, counts, above, cap, turns, True)
        slots = [turn_over(p, "sub", sub_count, t[0]) if t[0] else p for p, t in zip(packed, turns)]
        early = [n for n in range(len(turns)) if turns[n][3]]
        late = [n for n in range(len(turns)) if turns[n][2] > turns[n][1]]
        late.sort(key=lambda n: turn_order(sub_count, LATE_ORDER).index(turns[n][0]))
        above_places = [(i, turns[n][2] - turns[n][1], 0, kept, turns[n][0]) for i, n in enumerate(early)]
        places = [(i, 0, turns[n][1], turns[n][2], turns[n][0]) for i, n in enumerate(late)]
        early, late = [slots[n] for n in early], [slots[n] for n in late]
    else:
        regrouped = coefficients.reshape(vec_count, slice_cols, coefficients.shape[1])
        regrouped = lax.all_to_all(regrouped, "vec", split_axis=0, concat_axis=0, tiled=True)
        turns = [(k, 0, cap, 1) for k in range(sub_count)]
        slots = pack(sep, list(regrouped), list(range(vec_count)), counts, above, cap, turns, False)
        slots = lax.all_to_all(jnp.stack(slots), "sub", split_axis=0, concat_axis=0, tiled=True)
        early = late = [slots.reshape(group, cap + kept)]
        above_places, places = [(0, cap, 0, kept, None)], [(0, 0, 0, cap, None)]
    total, own = above_fields(early, above_places, group, sep, masked)
    return interior(late, places, group, count, interior_modes, total), own


def solution(mesh):
    placed = (P("sub", "vec"), P(), P(), P("sub", None), P(), P("sub", None), P("sub", None, None))
    return jax.shard_map(
        body,
        mesh=mesh,
        in_specs=placed,
        out_specs=(P("sub", "vec"), P("sub", "vec")),
        check_vma=False,
    )
```

```python
import functools

import jax
import jax.numpy as jnp
from jax import lax
from jax.experimental import pallas as pl
from jax.experimental.pallas import tpu as pltpu
from jax.sharding import PartitionSpec as P

BW = 256
SEPM = 128
LEVELS = 3
LANES = 128
ROWS = 16
EARLY_ORDER = [0, 4, 3, 1, 2, 6, 5, 7]
CUT = (4, 6)
LATE_ORDER = [0, 4, 5, 6, 1, 3, 2, 7]
PART = 128
VEC_ORDER = [2, 1, 3, 0]
AHEAD = 6 << 30
CONTRACT = (((1,), (1,)), ((), ()))


def turn_over(block, axis, count, turn):
    return lax.ppermute(block, axis, [(i, i ^ turn) for i in range(count)])


def split_kernel(coef_ref, *refs):
    count = len(refs) - 1
    sems = refs[count]
    slice_cols = refs[0].shape[0]
    me = lax.axis_index("vec")
    copies = []
    for k in list(range(1, count)) + [0]:
        at = pl.multiple_of(jnp.bitwise_xor(me, k) * slice_cols, slice_cols)
        copy = pltpu.make_async_copy(coef_ref.at[pl.ds(at, slice_cols)], refs[k], sems.at[k])
        copy.start()
        copies.append(copy)
    for copy in copies:
        copy.wait()


def split(coefficients, count):
    shape = (coefficients.shape[0] // count, coefficients.shape[1])
    return pl.pallas_call(
        split_kernel,
        out_shape=[jax.ShapeDtypeStruct(shape, coefficients.dtype)] * count,
        in_specs=[pl.BlockSpec(memory_space=pl.ANY)],
        out_specs=[pl.BlockSpec(memory_space=pltpu.VMEM)] * count,
        scratch_shapes=[pltpu.SemaphoreType.DMA((count,))],
        compiler_params=pltpu.CompilerParams(vmem_limit_bytes=4 << 20),
        cost_estimate=pl.CostEstimate(flops=AHEAD, transcendentals=0, bytes_accessed=1 << 20),
        name="split_slices",
    )(coefficients)


def put_windows(rows_ref, out_ref, count, offset, first, last, lane):
    start = offset // LANES
    shift = offset - start * LANES
    back = lax.rem(LANES - shift, LANES)
    base = pl.multiple_of(start * LANES, LANES)
    keep = lane < LANES - shift
    pieces = {}
    for j in range(first // LANES, last // LANES + 1):
        piece = rows_ref[:, pl.ds(base + j * LANES, LANES)].astype(jnp.float32)
        pieces[j] = pltpu.roll(piece, back, 1)
    for j in range(first // LANES, last // LANES):
        merged = jnp.where(keep, pieces[j], pieces[j + 1])
        merged = jnp.where(lane + j * LANES < count, merged, 0.0)
        at = j * LANES - first
        out_ref[:, at : at + LANES] = merged.astype(rows_ref.dtype)


def put_separators(from_ref, first, out_ref, to, owner, anc_ref):
    labels = [owner] + [anc_ref[l, owner] for l in range(LEVELS)]
    for n, label in enumerate(labels):
        at = pl.multiple_of(first + label * SEPM, SEPM)
        out_ref[:, to + n * SEPM : to + (n + 1) * SEPM] = from_ref[:, pl.ds(at, SEPM)]


def window_start(counts_ref, sub_count, owner):
    offset = jnp.int32(0)
    for p in range(sub_count):
        offset = offset + jnp.where(p < owner, counts_ref[p], 0)
    return offset


def pack_kernel(interior_total, cap, turns, direct, chunk_turns, counts_ref, anc_ref, *refs):
    sub_count = counts_ref.shape[0]
    chunks, outs, rows_ref = refs[1 : -len(turns) - 1], refs[-len(turns) - 1 : -1], refs[-1]
    slice_cols, width = chunks[0].shape
    total = len(chunks) * width
    mine = lax.axis_index("vec") if direct else jnp.int32(0)
    sub = lax.axis_index("sub") if direct else jnp.int32(0)
    for chunk, turn in zip(chunks, chunk_turns):
        at = pl.multiple_of(jnp.bitwise_xor(mine, turn) * width, LANES)
        rows_ref[:, pl.ds(at, width)] = chunk[...]
    if rows_ref.shape[1] > total:
        rows_ref[:, total:] = jnp.zeros((slice_cols, rows_ref.shape[1] - total), rows_ref.dtype)
    lane = lax.broadcasted_iota(jnp.int32, (slice_cols, LANES), 1)
    for out_ref, (turn, first, last, has_separators) in zip(outs, turns):
        owner = jnp.bitwise_xor(sub, turn)
        if last > first:
            offset = window_start(counts_ref, sub_count, owner)
            put_windows(rows_ref, out_ref, counts_ref[owner], offset, first, last, lane)
        if has_separators:
            put_separators(rows_ref, interior_total, out_ref, last - first, owner, anc_ref)


def pack(token, chunks, chunk_turns, row_counts, ancestors, cap, turns, direct):
    slice_cols, width = chunks[0].shape
    dtype = chunks[0].dtype
    sub_count = row_counts.shape[0]
    total = len(chunks) * width
    interior_total = total - sub_count * SEPM
    kept = (LEVELS + 1) * SEPM
    smem, vmem = pl.BlockSpec(memory_space=pltpu.SMEM), pl.BlockSpec(memory_space=pltpu.VMEM)
    return pl.pallas_call(
        functools.partial(pack_kernel, interior_total, cap, turns, direct, chunk_turns),
        out_shape=[jax.ShapeDtypeStruct((slice_cols, b - a + kept * c), dtype) for _, a, b, c in turns],
        in_specs=[smem, smem, pl.BlockSpec(memory_space=pl.ANY)] + [vmem] * len(chunks),
        out_specs=[vmem] * len(turns),
        scratch_shapes=[pltpu.VMEM((slice_cols, max(total, interior_total + cap)), dtype)],
        compiler_params=pltpu.CompilerParams(vmem_limit_bytes=8 << 20),
        name="pack_windows",
    )(row_counts, ancestors, token, *chunks)


def mask_kernel(
    counts_ref, anc_ref, pattern_ref, sep_ref, coupling_ref, sep_out, coupling_out, count_out
):
    me = lax.axis_index("sub")
    count_out[...] = jnp.full(count_out.shape, counts_ref[me], jnp.int32)
    for k in range(LEVELS + 1):
        label = me if k == 0 else anc_ref[k - 1, me]
        at = pl.multiple_of(label * BW, BW)
        sep_out[k * BW : (k + 1) * BW, :] = sep_ref[pl.ds(at, BW), :]
    for b in range(coupling_ref.shape[0] // BW):
        for l in range(LEVELS):
            live = pattern_ref[l, 0, b] != 0
            at = (slice(b * BW, (b + 1) * BW), slice(l * BW, (l + 1) * BW))
            part = coupling_ref[at]
            coupling_out[at] = jnp.where(live, part, jnp.zeros_like(part))


def mask(row_counts, ancestors, pattern, separator_modes, coupling):
    smem, vmem = pl.BlockSpec(memory_space=pltpu.SMEM), pl.BlockSpec(memory_space=pltpu.VMEM)
    return pl.pallas_call(
        mask_kernel,
        out_shape=(
            pltpu.VMEM(((LEVELS + 1) * BW, SEPM), coupling.dtype),
            pltpu.VMEM(coupling.shape, coupling.dtype),
            pltpu.VMEM((8, LANES), jnp.int32),
        ),
        in_specs=[smem, smem, smem, vmem, vmem],
        out_specs=(vmem, vmem, vmem),
        compiler_params=pltpu.CompilerParams(vmem_limit_bytes=4 << 20),
        cost_estimate=pl.CostEstimate(flops=0, transcendentals=0, bytes_accessed=2 * coupling.size),
        name="mask_coupling",
    )(row_counts, ancestors, pattern, separator_modes, coupling)


def gather_rows(places, slots, got_ref):
    for n, lanes, first, last, turn in places:
        slice_cols = slots[n].shape[0]
        block = 0 if turn is None else jnp.bitwise_xor(lax.axis_index("sub"), turn)
        at = pl.multiple_of(block * slice_cols, slice_cols)
        got_ref[pl.ds(at, slice_cols), first:last] = slots[n][:, lanes : lanes + last - first]


def above_kernel(rows, places, slot_count, *refs):
    slots, (sep_ref, coupling_ref, total_ref, own_ref, got_ref, above_ref) = refs[:slot_count], refs[slot_count:]
    gather_rows(places, slots, got_ref)
    for k in range(LEVELS + 1):
        part = got_ref[:, k * SEPM : (k + 1) * SEPM]
        block = lax.dot_general(
            sep_ref[k * BW : (k + 1) * BW, :], part, CONTRACT, preferred_element_type=jnp.float32
        ).astype(jnp.bfloat16)
        if k == 0:
            own_ref[...] = block
        else:
            above_ref[(k - 1) * BW : k * BW, :] = block
    for s in range(coupling_ref.shape[0] // rows):
        at = slice(s * rows, (s + 1) * rows)
        total_ref[at, :] = jnp.dot(
            coupling_ref[at, :], above_ref[...], preferred_element_type=jnp.float32
        )


def above_fields(slots, places, group, sep, coupling):
    phys = coupling.shape[0]
    vmem = pl.BlockSpec(memory_space=pltpu.VMEM)
    return pl.pallas_call(
        functools.partial(above_kernel, 2 * BW, places, len(slots)),
        out_shape=(
            pltpu.VMEM((phys, group), jnp.float32),
            jax.ShapeDtypeStruct((BW, group), jnp.bfloat16),
        ),
        in_specs=[vmem] * (len(slots) + 2),
        out_specs=(vmem, vmem),
        scratch_shapes=[
            pltpu.VMEM((group, (LEVELS + 1) * SEPM), jnp.bfloat16),
            pltpu.VMEM((LEVELS * BW, group), jnp.bfloat16),
        ],
        compiler_params=pltpu.CompilerParams(vmem_limit_bytes=4 << 20),
        cost_estimate=pl.CostEstimate(
            flops=2 * coupling.size * group, transcendentals=0, bytes_accessed=2 * coupling.size
        ),
        name="separator_fields_and_coupling",
    )(*slots, sep, coupling)


def interior_kernel(rows, places, slot_count, *refs):
    slots, refs = refs[:slot_count], refs[slot_count:]
    count_ref, modes_ref, total_ref, field_ref, got_ref, coef_ref, block_ref, sems = refs
    phys, cap = modes_ref.shape
    tiles = jnp.clip((jnp.max(count_ref[...]) + BW - 1) // BW, 1, cap // BW)
    gather_rows(places, slots, got_ref)
    copies = [
        pltpu.make_async_copy(block_ref.at[pl.ds(at, rows)], field_ref.at[pl.ds(at, rows)], sems.at[n])
        for n, at in enumerate(range(0, phys, rows))
    ]
    for used in range(1, cap // BW + 1):

        @pl.when(tiles == used)
        def _(depth=used * BW):
            coef_ref[:depth, :] = got_ref[:, :depth].T
            for n, first in enumerate(range(0, phys, rows)):
                at = slice(first, first + rows)
                acc = jnp.dot(
                    modes_ref[at, :depth], coef_ref[:depth, :], preferred_element_type=jnp.float32
                )
                block_ref[at, :] = (acc + total_ref[at, :]).astype(block_ref.dtype)
                copies[n].start()

    for copy in copies:
        copy.wait()


def interior(slots, places, group, count, modes, total):
    phys, cap = modes.shape
    rows = 2 * BW
    vmem = pl.BlockSpec(memory_space=pltpu.VMEM)
    return pl.pallas_call(
        functools.partial(interior_kernel, rows, places, len(slots)),
        out_shape=jax.ShapeDtypeStruct((phys, group), jnp.bfloat16),
        in_specs=[vmem] * (len(slots) + 3),
        out_specs=pl.BlockSpec(memory_space=pl.ANY),
        scratch_shapes=[
            pltpu.VMEM((group, cap), jnp.bfloat16),
            pltpu.VMEM((cap, group), jnp.bfloat16),
            pltpu.VMEM((phys, group), jnp.bfloat16),
            pltpu.SemaphoreType.DMA((phys // rows,)),
        ],
        compiler_params=pltpu.CompilerParams(vmem_limit_bytes=8 << 20),
        name="interior_field",
    )(*slots, count, modes, total)


def in_hbm(array):
    return pltpu.with_memory_space_constraint(array, pltpu.HBM)


def turn_order(count, order):
    return order if count == len(order) else list(range(count))


def body(coefficients, row_counts, ancestors, interior_modes, separator_modes, coupling, pattern):
    vec_count, sub_count = lax.axis_size("vec"), lax.axis_size("sub")
    slice_cols = coefficients.shape[0] // vec_count
    group = slice_cols * sub_count
    cap = interior_modes.shape[1]
    kept = (LEVELS + 1) * SEPM
    counts = in_hbm(row_counts)
    above = in_hbm(ancestors.T)
    gates = in_hbm(jnp.transpose(pattern, (2, 0, 1)))
    sep, masked, count = mask(counts, above, gates, separator_modes, coupling)
    powers = vec_count & (vec_count - 1) == 0 and sub_count & (sub_count - 1) == 0
    if powers and sub_count > 1 and slice_cols % ROWS == 0:
        blocks = split(in_hbm(coefficients), vec_count)
        chunk_turns = turn_order(vec_count, VEC_ORDER)
        chunks = [turn_over(blocks[k], "vec", vec_count, k) if k else blocks[0] for k in chunk_turns]
        turns = []
        for k in turn_order(sub_count, EARLY_ORDER):
            part = min(PART, cap)
            turns += [(k, 0, part, 1), (k, part, cap, 0)] if k in CUT else [(k, 0, cap, 1)]
        packed = pack(sep, chunks, chunk_turns, counts, above, cap, turns, True)
        slots = [turn_over(p, "sub", sub_count, t[0]) if t[0] else p for p, t in zip(packed, turns)]
        early = [n for n in range(len(turns)) if turns[n][3]]
        late = [n for n in range(len(turns)) if turns[n][2] > turns[n][1]]
        late.sort(key=lambda n: turn_order(sub_count, LATE_ORDER).index(turns[n][0]))
        above_places = [(i, turns[n][2] - turns[n][1], 0, kept, turns[n][0]) for i, n in enumerate(early)]
        places = [(i, 0, turns[n][1], turns[n][2], turns[n][0]) for i, n in enumerate(late)]
        early, late = [slots[n] for n in early], [slots[n] for n in late]
    else:
        regrouped = coefficients.reshape(vec_count, slice_cols, coefficients.shape[1])
        regrouped = lax.all_to_all(regrouped, "vec", split_axis=0, concat_axis=0, tiled=True)
        turns = [(k, 0, cap, 1) for k in range(sub_count)]
        slots = pack(sep, list(regrouped), list(range(vec_count)), counts, above, cap, turns, False)
        slots = lax.all_to_all(jnp.stack(slots), "sub", split_axis=0, concat_axis=0, tiled=True)
        early = late = [slots.reshape(group, cap + kept)]
        above_places, places = [(0, cap, 0, kept, None)], [(0, 0, 0, cap, None)]
    total, own = above_fields(early, above_places, group, sep, masked)
    return interior(late, places, group, count, interior_modes, total), own


def solution(mesh):
    placed = (P("sub", "vec"), P(), P(), P("sub", None), P(), P("sub", None), P("sub", None, None))
    return jax.shard_map(
        body,
        mesh=mesh,
        in_specs=placed,
        out_specs=(P("sub", "vec"), P("sub", "vec")),
        check_vma=False,
    )
```

```python
import functools

import jax
import jax.numpy as jnp
from jax import lax
from jax.experimental import pallas as pl
from jax.experimental.pallas import tpu as pltpu
from jax.sharding import PartitionSpec as P

BW = 256
SEPM = 128
LEVELS = 3
LANES = 128
ROWS = 16
EARLY_ORDER = [0, 4, 3, 1, 2, 6, 5, 7]
CUT = (4, 6)
LATE_ORDER = [0, 4, 5, 6, 1, 3, 2, 7]
PART = 128
VEC_ORDER = [2, 1, 3, 0]
AHEAD = 6 << 30
CONTRACT = (((1,), (1,)), ((), ()))


def turn_over(block, axis, count, turn):
    return lax.ppermute(block, axis, [(i, i ^ turn) for i in range(count)])


def split_kernel(coef_ref, *refs):
    count = len(refs) - 1
    sems = refs[count]
    slice_cols = refs[0].shape[0]
    me = lax.axis_index("vec")
    copies = []
    for k in list(range(1, count)) + [0]:
        at = pl.multiple_of(jnp.bitwise_xor(me, k) * slice_cols, slice_cols)
        copy = pltpu.make_async_copy(coef_ref.at[pl.ds(at, slice_cols)], refs[k], sems.at[k])
        copy.start()
        copies.append(copy)
    for copy in copies:
        copy.wait()


def split(coefficients, count):
    shape = (coefficients.shape[0] // count, coefficients.shape[1])
    return pl.pallas_call(
        split_kernel,
        out_shape=[jax.ShapeDtypeStruct(shape, coefficients.dtype)] * count,
        in_specs=[pl.BlockSpec(memory_space=pl.ANY)],
        out_specs=[pl.BlockSpec(memory_space=pltpu.VMEM)] * count,
        scratch_shapes=[pltpu.SemaphoreType.DMA((count,))],
        compiler_params=pltpu.CompilerParams(vmem_limit_bytes=4 << 20),
        cost_estimate=pl.CostEstimate(flops=AHEAD, transcendentals=0, bytes_accessed=1 << 20),
        name="split_slices",
    )(coefficients)


def put_windows(rows_ref, out_ref, count, offset, first, last, lane):
    start = offset // LANES
    shift = offset - start * LANES
    back = lax.rem(LANES - shift, LANES)
    base = pl.multiple_of(start * LANES, LANES)
    keep = lane < LANES - shift
    pieces = {}
    for j in range(first // LANES, last // LANES + 1):
        piece = rows_ref[:, pl.ds(base + j * LANES, LANES)]
        pieces[j] = pltpu.roll(piece, back, 1)
    for j in range(first // LANES, last // LANES):
        merged = jnp.where(keep, pieces[j], pieces[j + 1])
        merged = jnp.where(lane + j * LANES < count, merged, jnp.zeros_like(merged))
        at = j * LANES - first
        out_ref[:, at : at + LANES] = merged


def put_separators(from_ref, first, out_ref, to, owner, anc_ref):
    labels = [owner] + [anc_ref[l, owner] for l in range(LEVELS)]
    for n, label in enumerate(labels):
        at = pl.multiple_of(first + label * SEPM, SEPM)
        out_ref[:, to + n * SEPM : to + (n + 1) * SEPM] = from_ref[:, pl.ds(at, SEPM)]


def window_start(counts_ref, sub_count, owner):
    offset = jnp.int32(0)
    for p in range(sub_count):
        offset = offset + jnp.where(p < owner, counts_ref[p], 0)
    return offset


def pack_kernel(interior_total, cap, turns, direct, chunk_turns, counts_ref, anc_ref, *refs):
    sub_count = counts_ref.shape[0]
    chunks, outs, rows_ref = refs[1 : -len(turns) - 1], refs[-len(turns) - 1 : -1], refs[-1]
    slice_cols, width = chunks[0].shape
    total = len(chunks) * width
    mine = lax.axis_index("vec") if direct else jnp.int32(0)
    sub = lax.axis_index("sub") if direct else jnp.int32(0)
    for chunk, turn in zip(chunks, chunk_turns):
        at = pl.multiple_of(jnp.bitwise_xor(mine, turn) * width, LANES)
        rows_ref[:, pl.ds(at, width)] = chunk[...]
    if rows_ref.shape[1] > total:
        rows_ref[:, total:] = jnp.zeros((slice_cols, rows_ref.shape[1] - total), rows_ref.dtype)
    lane = lax.broadcasted_iota(jnp.int32, (slice_cols, LANES), 1)
    for out_ref, (turn, first, last, has_separators) in zip(outs, turns):
        owner = jnp.bitwise_xor(sub, turn)
        if last > first:
            offset = window_start(counts_ref, sub_count, owner)
            put_windows(rows_ref, out_ref, counts_ref[owner], offset, first, last, lane)
        if has_separators:
            put_separators(rows_ref, interior_total, out_ref, last - first, owner, anc_ref)


def pack(token, chunks, chunk_turns, row_counts, ancestors, cap, turns, direct):
    slice_cols, width = chunks[0].shape
    dtype = chunks[0].dtype
    sub_count = row_counts.shape[0]
    total = len(chunks) * width
    interior_total = total - sub_count * SEPM
    kept = (LEVELS + 1) * SEPM
    smem, vmem = pl.BlockSpec(memory_space=pltpu.SMEM), pl.BlockSpec(memory_space=pltpu.VMEM)
    return pl.pallas_call(
        functools.partial(pack_kernel, interior_total, cap, turns, direct, chunk_turns),
        out_shape=[jax.ShapeDtypeStruct((slice_cols, b - a + kept * c), dtype) for _, a, b, c in turns],
        in_specs=[smem, smem, pl.BlockSpec(memory_space=pl.ANY)] + [vmem] * len(chunks),
        out_specs=[vmem] * len(turns),
        scratch_shapes=[pltpu.VMEM((slice_cols, max(total, interior_total + cap)), dtype)],
        compiler_params=pltpu.CompilerParams(vmem_limit_bytes=8 << 20),
        name="pack_windows",
    )(row_counts, ancestors, token, *chunks)


def mask_kernel(
    counts_ref, anc_ref, pattern_ref, sep_ref, coupling_ref, sep_out, coupling_out, count_out
):
    me = lax.axis_index("sub")
    count_out[...] = jnp.full(count_out.shape, counts_ref[me], jnp.int32)
    for k in range(LEVELS + 1):
        label = me if k == 0 else anc_ref[k - 1, me]
        at = pl.multiple_of(label * BW, BW)
        sep_out[k * BW : (k + 1) * BW, :] = sep_ref[pl.ds(at, BW), :]
    for b in range(coupling_ref.shape[0] // BW):
        for l in range(LEVELS):
            live = pattern_ref[l, 0, b] != 0
            at = (slice(b * BW, (b + 1) * BW), slice(l * BW, (l + 1) * BW))
            part = coupling_ref[at]
            coupling_out[at] = jnp.where(live, part, jnp.zeros_like(part))


def mask(row_counts, ancestors, pattern, separator_modes, coupling):
    smem, vmem = pl.BlockSpec(memory_space=pltpu.SMEM), pl.BlockSpec(memory_space=pltpu.VMEM)
    return pl.pallas_call(
        mask_kernel,
        out_shape=(
            pltpu.VMEM(((LEVELS + 1) * BW, SEPM), coupling.dtype),
            pltpu.VMEM(coupling.shape, coupling.dtype),
            pltpu.VMEM((8, LANES), jnp.int32),
        ),
        in_specs=[smem, smem, smem, vmem, vmem],
        out_specs=(vmem, vmem, vmem),
        compiler_params=pltpu.CompilerParams(vmem_limit_bytes=4 << 20),
        cost_estimate=pl.CostEstimate(flops=0, transcendentals=0, bytes_accessed=2 * coupling.size),
        name="mask_coupling",
    )(row_counts, ancestors, pattern, separator_modes, coupling)


def gather_rows(places, slots, got_ref, limit):
    for n, lanes, first, last, turn in places:
        last = min(last, limit)
        if last <= first:
            continue
        slice_cols = slots[n].shape[0]
        block = 0 if turn is None else jnp.bitwise_xor(lax.axis_index("sub"), turn)
        at = pl.multiple_of(block * slice_cols, slice_cols)
        got_ref[pl.ds(at, slice_cols), first:last] = slots[n][:, lanes : lanes + last - first]


def above_kernel(rows, places, slot_count, *refs):
    slots, (sep_ref, coupling_ref, total_ref, own_ref, got_ref, above_ref) = refs[:slot_count], refs[slot_count:]
    gather_rows(places, slots, got_ref, got_ref.shape[1])
    for k in range(LEVELS + 1):
        part = got_ref[:, k * SEPM : (k + 1) * SEPM]
        block = lax.dot_general(
            sep_ref[k * BW : (k + 1) * BW, :], part, CONTRACT, preferred_element_type=jnp.float32
        ).astype(jnp.bfloat16)
        if k == 0:
            own_ref[...] = block
        else:
            above_ref[(k - 1) * BW : k * BW, :] = block
    for s in range(coupling_ref.shape[0] // rows):
        at = slice(s * rows, (s + 1) * rows)
        total_ref[at, :] = jnp.dot(
            coupling_ref[at, :], above_ref[...], preferred_element_type=jnp.float32
        )


def above_fields(slots, places, group, sep, coupling):
    phys = coupling.shape[0]
    vmem = pl.BlockSpec(memory_space=pltpu.VMEM)
    return pl.pallas_call(
        functools.partial(above_kernel, 2 * BW, places, len(slots)),
        out_shape=(
            pltpu.VMEM((phys, group), jnp.float32),
            jax.ShapeDtypeStruct((BW, group), jnp.bfloat16),
        ),
        in_specs=[vmem] * (len(slots) + 2),
        out_specs=(vmem, vmem),
        scratch_shapes=[
            pltpu.VMEM((group, (LEVELS + 1) * SEPM), jnp.bfloat16),
            pltpu.VMEM((LEVELS * BW, group), jnp.bfloat16),
        ],
        compiler_params=pltpu.CompilerParams(vmem_limit_bytes=4 << 20),
        cost_estimate=pl.CostEstimate(
            flops=2 * coupling.size * group, transcendentals=0, bytes_accessed=2 * coupling.size
        ),
        name="separator_fields_and_coupling",
    )(*slots, sep, coupling)


def interior_kernel(rows, places, slot_count, *refs):
    slots, refs = refs[:slot_count], refs[slot_count:]
    count_ref, modes_ref, total_ref, field_ref, got_ref, coef_ref, block_ref, sems = refs
    phys, cap = modes_ref.shape
    tiles = jnp.clip((jnp.max(count_ref[...]) + BW - 1) // BW, 1, cap // BW)
    copies = [
        pltpu.make_async_copy(block_ref.at[pl.ds(at, rows)], field_ref.at[pl.ds(at, rows)], sems.at[n])
        for n, at in enumerate(range(0, phys, rows))
    ]
    for used in range(1, cap // BW + 1):

        @pl.when(tiles == used)
        def _(depth=used * BW):
            gather_rows(places, slots, got_ref, depth)
            coef_ref[:depth, :] = got_ref[:, :depth].T
            for n, first in enumerate(range(0, phys, rows)):
                at = slice(first, first + rows)
                acc = jnp.dot(
                    modes_ref[at, :depth], coef_ref[:depth, :], preferred_element_type=jnp.float32
                )
                block_ref[at, :] = (acc + total_ref[at, :]).astype(block_ref.dtype)
                copies[n].start()

    for copy in copies:
        copy.wait()


def interior(slots, places, group, count, modes, total):
    phys, cap = modes.shape
    rows = 2 * BW
    vmem = pl.BlockSpec(memory_space=pltpu.VMEM)
    return pl.pallas_call(
        functools.partial(interior_kernel, rows, places, len(slots)),
        out_shape=jax.ShapeDtypeStruct((phys, group), jnp.bfloat16),
        in_specs=[vmem] * (len(slots) + 3),
        out_specs=pl.BlockSpec(memory_space=pl.ANY),
        scratch_shapes=[
            pltpu.VMEM((group, cap), jnp.bfloat16),
            pltpu.VMEM((cap, group), jnp.bfloat16),
            pltpu.VMEM((phys, group), jnp.bfloat16),
            pltpu.SemaphoreType.DMA((phys // rows,)),
        ],
        compiler_params=pltpu.CompilerParams(vmem_limit_bytes=8 << 20),
        name="interior_field",
    )(*slots, count, modes, total)


def in_hbm(array):
    return pltpu.with_memory_space_constraint(array, pltpu.HBM)


def turn_order(count, order):
    return order if count == len(order) else list(range(count))


def body(coefficients, row_counts, ancestors, interior_modes, separator_modes, coupling, pattern):
    vec_count, sub_count = lax.axis_size("vec"), lax.axis_size("sub")
    slice_cols = coefficients.shape[0] // vec_count
    group = slice_cols * sub_count
    cap = interior_modes.shape[1]
    kept = (LEVELS + 1) * SEPM
    counts = in_hbm(row_counts)
    above = in_hbm(ancestors.T)
    gates = in_hbm(jnp.transpose(pattern, (2, 0, 1)))
    sep, masked, count = mask(counts, above, gates, separator_modes, coupling)
    powers = vec_count & (vec_count - 1) == 0 and sub_count & (sub_count - 1) == 0
    if powers and sub_count > 1 and slice_cols % ROWS == 0:
        blocks = split(in_hbm(coefficients), vec_count)
        chunk_turns = turn_order(vec_count, VEC_ORDER)
        chunks = [turn_over(blocks[k], "vec", vec_count, k) if k else blocks[0] for k in chunk_turns]
        turns = []
        for k in turn_order(sub_count, EARLY_ORDER):
            part = min(PART, cap)
            turns += [(k, 0, part, 1), (k, part, cap, 0)] if k in CUT else [(k, 0, cap, 1)]
        packed = pack(sep, chunks, chunk_turns, counts, above, cap, turns, True)
        slots = [turn_over(p, "sub", sub_count, t[0]) if t[0] else p for p, t in zip(packed, turns)]
        early = [n for n in range(len(turns)) if turns[n][3]]
        late = [n for n in range(len(turns)) if turns[n][2] > turns[n][1]]
        late.sort(key=lambda n: turn_order(sub_count, LATE_ORDER).index(turns[n][0]))
        above_places = [(i, turns[n][2] - turns[n][1], 0, kept, turns[n][0]) for i, n in enumerate(early)]
        places = [(i, 0, turns[n][1], turns[n][2], turns[n][0]) for i, n in enumerate(late)]
        early, late = [slots[n] for n in early], [slots[n] for n in late]
    else:
        regrouped = coefficients.reshape(vec_count, slice_cols, coefficients.shape[1])
        regrouped = lax.all_to_all(regrouped, "vec", split_axis=0, concat_axis=0, tiled=True)
        turns = [(k, 0, cap, 1) for k in range(sub_count)]
        slots = pack(sep, list(regrouped), list(range(vec_count)), counts, above, cap, turns, False)
        slots = lax.all_to_all(jnp.stack(slots), "sub", split_axis=0, concat_axis=0, tiled=True)
        early = late = [slots.reshape(group, cap + kept)]
        above_places, places = [(0, cap, 0, kept, None)], [(0, 0, 0, cap, None)]
    total, own = above_fields(early, above_places, group, sep, masked)
    return interior(late, places, group, count, interior_modes, total), own


def solution(mesh):
    placed = (P("sub", "vec"), P(), P(), P("sub", None), P(), P("sub", None), P("sub", None, None))
    return jax.shard_map(
        body,
        mesh=mesh,
        in_specs=placed,
        out_specs=(P("sub", "vec"), P("sub", "vec")),
        check_vma=False,
    )
```

```python
import functools

import jax
import jax.numpy as jnp
from jax import lax
from jax.experimental import pallas as pl
from jax.experimental.pallas import tpu as pltpu
from jax.sharding import PartitionSpec as P

BW = 256
SEPM = 128
LEVELS = 3
LANES = 128
ROWS = 16
EARLY_ORDER = [0, 4, 6, 1, 2, 3, 5, 7]
CUT = (4, 6)
LATE_ORDER = [0, 4, 5, 6, 1, 3, 2, 7]
PART = 128
VEC_ORDER = [2, 1, 3, 0]
AHEAD = 6 << 30
CONTRACT = (((1,), (1,)), ((), ()))


def turn_over(block, axis, count, turn):
    return lax.ppermute(block, axis, [(i, i ^ turn) for i in range(count)])


def split_kernel(coef_ref, *refs):
    count = len(refs) - 1
    sems = refs[count]
    slice_cols = refs[0].shape[0]
    me = lax.axis_index("vec")
    copies = []
    for k in list(range(1, count)) + [0]:
        at = pl.multiple_of(jnp.bitwise_xor(me, k) * slice_cols, slice_cols)
        copy = pltpu.make_async_copy(coef_ref.at[pl.ds(at, slice_cols)], refs[k], sems.at[k])
        copy.start()
        copies.append(copy)
    for copy in copies:
        copy.wait()


def split(coefficients, count):
    shape = (coefficients.shape[0] // count, coefficients.shape[1])
    return pl.pallas_call(
        split_kernel,
        out_shape=[jax.ShapeDtypeStruct(shape, coefficients.dtype)] * count,
        in_specs=[pl.BlockSpec(memory_space=pl.ANY)],
        out_specs=[pl.BlockSpec(memory_space=pltpu.VMEM)] * count,
        scratch_shapes=[pltpu.SemaphoreType.DMA((count,))],
        compiler_params=pltpu.CompilerParams(vmem_limit_bytes=4 << 20),
        cost_estimate=pl.CostEstimate(flops=AHEAD, transcendentals=0, bytes_accessed=1 << 20),
        name="split_slices",
    )(coefficients)


def put_windows(rows_ref, out_ref, count, offset, first, last, lane):
    start = offset // LANES
    shift = offset - start * LANES
    back = lax.rem(LANES - shift, LANES)
    base = pl.multiple_of(start * LANES, LANES)
    keep = lane < LANES - shift
    pieces = {}
    for j in range(first // LANES, last // LANES + 1):
        piece = rows_ref[:, pl.ds(base + j * LANES, LANES)].astype(jnp.float32)
        pieces[j] = pltpu.roll(piece, back, 1)
    for j in range(first // LANES, last // LANES):
        merged = jnp.where(keep, pieces[j], pieces[j + 1])
        merged = jnp.where(lane + j * LANES < count, merged, 0.0)
        at = j * LANES - first
        out_ref[:, at : at + LANES] = merged.astype(rows_ref.dtype)


def put_separators(from_ref, first, out_ref, to, owner, anc_ref):
    labels = [owner] + [anc_ref[l, owner] for l in range(LEVELS)]
    for n, label in enumerate(labels):
        at = pl.multiple_of(first + label * SEPM, SEPM)
        out_ref[:, to + n * SEPM : to + (n + 1) * SEPM] = from_ref[:, pl.ds(at, SEPM)]


def window_start(counts_ref, sub_count, owner):
    offset = jnp.int32(0)
    for p in range(sub_count):
        offset = offset + jnp.where(p < owner, counts_ref[p], 0)
    return offset


def pack_kernel(interior_total, cap, turns, direct, chunk_turns, counts_ref, anc_ref, *refs):
    sub_count = counts_ref.shape[0]
    chunks, outs, rows_ref = refs[1 : -len(turns) - 1], refs[-len(turns) - 1 : -1], refs[-1]
    slice_cols, width = chunks[0].shape
    total = len(chunks) * width
    mine = lax.axis_index("vec") if direct else jnp.int32(0)
    sub = lax.axis_index("sub") if direct else jnp.int32(0)
    for chunk, turn in zip(chunks, chunk_turns):
        at = pl.multiple_of(jnp.bitwise_xor(mine, turn) * width, LANES)
        rows_ref[:, pl.ds(at, width)] = chunk[...]
    if rows_ref.shape[1] > total:
        rows_ref[:, total:] = jnp.zeros((slice_cols, rows_ref.shape[1] - total), rows_ref.dtype)
    lane = lax.broadcasted_iota(jnp.int32, (slice_cols, LANES), 1)
    for out_ref, (turn, first, last, has_separators) in zip(outs, turns):
        owner = jnp.bitwise_xor(sub, turn)
        if last > first:
            offset = window_start(counts_ref, sub_count, owner)
            put_windows(rows_ref, out_ref, counts_ref[owner], offset, first, last, lane)
        if has_separators:
            put_separators(rows_ref, interior_total, out_ref, last - first, owner, anc_ref)


def pack(token, chunks, chunk_turns, row_counts, ancestors, cap, turns, direct):
    slice_cols, width = chunks[0].shape
    dtype = chunks[0].dtype
    sub_count = row_counts.shape[0]
    total = len(chunks) * width
    interior_total = total - sub_count * SEPM
    kept = (LEVELS + 1) * SEPM
    smem, vmem = pl.BlockSpec(memory_space=pltpu.SMEM), pl.BlockSpec(memory_space=pltpu.VMEM)
    return pl.pallas_call(
        functools.partial(pack_kernel, interior_total, cap, turns, direct, chunk_turns),
        out_shape=[jax.ShapeDtypeStruct((slice_cols, b - a + kept * c), dtype) for _, a, b, c in turns],
        in_specs=[smem, smem, pl.BlockSpec(memory_space=pl.ANY)] + [vmem] * len(chunks),
        out_specs=[vmem] * len(turns),
        scratch_shapes=[pltpu.VMEM((slice_cols, max(total, interior_total + cap)), dtype)],
        compiler_params=pltpu.CompilerParams(vmem_limit_bytes=8 << 20),
        name="pack_windows",
    )(row_counts, ancestors, token, *chunks)


def mask_kernel(
    counts_ref, anc_ref, pattern_ref, sep_ref, coupling_ref, sep_out, coupling_out, count_out
):
    me = lax.axis_index("sub")
    count_out[...] = jnp.full(count_out.shape, counts_ref[me], jnp.int32)
    for k in range(LEVELS + 1):
        label = me if k == 0 else anc_ref[k - 1, me]
        at = pl.multiple_of(label * BW, BW)
        sep_out[k * BW : (k + 1) * BW, :] = sep_ref[pl.ds(at, BW), :]
    for b in range(coupling_ref.shape[0] // BW):
        for l in range(LEVELS):
            live = pattern_ref[l, 0, b] != 0
            at = (slice(b * BW, (b + 1) * BW), slice(l * BW, (l + 1) * BW))
            part = coupling_ref[at]
            coupling_out[at] = jnp.where(live, part, jnp.zeros_like(part))


def mask(row_counts, ancestors, pattern, separator_modes, coupling):
    smem, vmem = pl.BlockSpec(memory_space=pltpu.SMEM), pl.BlockSpec(memory_space=pltpu.VMEM)
    return pl.pallas_call(
        mask_kernel,
        out_shape=(
            pltpu.VMEM(((LEVELS + 1) * BW, SEPM), coupling.dtype),
            pltpu.VMEM(coupling.shape, coupling.dtype),
            pltpu.VMEM((8, LANES), jnp.int32),
        ),
        in_specs=[smem, smem, smem, vmem, vmem],
        out_specs=(vmem, vmem, vmem),
        compiler_params=pltpu.CompilerParams(vmem_limit_bytes=4 << 20),
        cost_estimate=pl.CostEstimate(flops=0, transcendentals=0, bytes_accessed=2 * coupling.size),
        name="mask_coupling",
    )(row_counts, ancestors, pattern, separator_modes, coupling)


def gather_rows(places, slots, got_ref):
    for n, lanes, first, last, turn in places:
        slice_cols = slots[n].shape[0]
        block = 0 if turn is None else jnp.bitwise_xor(lax.axis_index("sub"), turn)
        at = pl.multiple_of(block * slice_cols, slice_cols)
        got_ref[pl.ds(at, slice_cols), first:last] = slots[n][:, lanes : lanes + last - first]


def above_kernel(rows, places, slot_count, *refs):
    slots, (sep_ref, coupling_ref, total_ref, own_ref, got_ref, above_ref) = refs[:slot_count], refs[slot_count:]
    gather_rows(places, slots, got_ref)
    for k in range(LEVELS + 1):
        part = got_ref[:, k * SEPM : (k + 1) * SEPM]
        block = lax.dot_general(
            sep_ref[k * BW : (k + 1) * BW, :], part, CONTRACT, preferred_element_type=jnp.float32
        ).astype(jnp.bfloat16)
        if k == 0:
            own_ref[...] = block
        else:
            above_ref[(k - 1) * BW : k * BW, :] = block
    for s in range(coupling_ref.shape[0] // rows):
        at = slice(s * rows, (s + 1) * rows)
        total_ref[at, :] = jnp.dot(
            coupling_ref[at, :], above_ref[...], preferred_element_type=jnp.float32
        )


def above_fields(slots, places, group, sep, coupling):
    phys = coupling.shape[0]
    vmem = pl.BlockSpec(memory_space=pltpu.VMEM)
    return pl.pallas_call(
        functools.partial(above_kernel, 2 * BW, places, len(slots)),
        out_shape=(
            pltpu.VMEM((phys, group), jnp.float32),
            jax.ShapeDtypeStruct((BW, group), jnp.bfloat16),
        ),
        in_specs=[vmem] * (len(slots) + 2),
        out_specs=(vmem, vmem),
        scratch_shapes=[
            pltpu.VMEM((group, (LEVELS + 1) * SEPM), jnp.bfloat16),
            pltpu.VMEM((LEVELS * BW, group), jnp.bfloat16),
        ],
        compiler_params=pltpu.CompilerParams(vmem_limit_bytes=4 << 20),
        cost_estimate=pl.CostEstimate(
            flops=2 * coupling.size * group, transcendentals=0, bytes_accessed=2 * coupling.size
        ),
        name="separator_fields_and_coupling",
    )(*slots, sep, coupling)


def interior_kernel(rows, places, slot_count, *refs):
    slots, refs = refs[:slot_count], refs[slot_count:]
    count_ref, modes_ref, total_ref, field_ref, got_ref, coef_ref, block_ref, sems = refs
    phys, cap = modes_ref.shape
    tiles = jnp.clip((jnp.max(count_ref[...]) + BW - 1) // BW, 1, cap // BW)
    gather_rows(places, slots, got_ref)
    copies = [
        pltpu.make_async_copy(block_ref.at[pl.ds(at, rows)], field_ref.at[pl.ds(at, rows)], sems.at[n])
        for n, at in enumerate(range(0, phys, rows))
    ]
    for used in range(1, cap // BW + 1):

        @pl.when(tiles == used)
        def _(depth=used * BW):
            coef_ref[:depth, :] = got_ref[:, :depth].T
            for n, first in enumerate(range(0, phys, rows)):
                at = slice(first, first + rows)
                acc = jnp.dot(
                    modes_ref[at, :depth], coef_ref[:depth, :], preferred_element_type=jnp.float32
                )
                block_ref[at, :] = (acc + total_ref[at, :]).astype(block_ref.dtype)
                copies[n].start()

    for copy in copies:
        copy.wait()


def interior(slots, places, group, count, modes, total):
    phys, cap = modes.shape
    rows = 2 * BW
    vmem = pl.BlockSpec(memory_space=pltpu.VMEM)
    return pl.pallas_call(
        functools.partial(interior_kernel, rows, places, len(slots)),
        out_shape=jax.ShapeDtypeStruct((phys, group), jnp.bfloat16),
        in_specs=[vmem] * (len(slots) + 3),
        out_specs=pl.BlockSpec(memory_space=pl.ANY),
        scratch_shapes=[
            pltpu.VMEM((group, cap), jnp.bfloat16),
            pltpu.VMEM((cap, group), jnp.bfloat16),
            pltpu.VMEM((phys, group), jnp.bfloat16),
            pltpu.SemaphoreType.DMA((phys // rows,)),
        ],
        compiler_params=pltpu.CompilerParams(vmem_limit_bytes=8 << 20),
        name="interior_field",
    )(*slots, count, modes, total)


def in_hbm(array):
    return pltpu.with_memory_space_constraint(array, pltpu.HBM)


def turn_order(count, order):
    return order if count == len(order) else list(range(count))


def body(coefficients, row_counts, ancestors, interior_modes, separator_modes, coupling, pattern):
    vec_count, sub_count = lax.axis_size("vec"), lax.axis_size("sub")
    slice_cols = coefficients.shape[0] // vec_count
    group = slice_cols * sub_count
    cap = interior_modes.shape[1]
    kept = (LEVELS + 1) * SEPM
    counts = in_hbm(row_counts)
    above = in_hbm(ancestors.T)
    gates = in_hbm(jnp.transpose(pattern, (2, 0, 1)))
    sep, masked, count = mask(counts, above, gates, separator_modes, coupling)
    powers = vec_count & (vec_count - 1) == 0 and sub_count & (sub_count - 1) == 0
    if powers and sub_count > 1 and slice_cols % ROWS == 0:
        blocks = split(in_hbm(coefficients), vec_count)
        chunk_turns = turn_order(vec_count, VEC_ORDER)
        chunks = [turn_over(blocks[k], "vec", vec_count, k) if k else blocks[0] for k in chunk_turns]
        turns = []
        for k in turn_order(sub_count, EARLY_ORDER):
            part = min(PART, cap)
            turns += [(k, 0, part, 1), (k, part, cap, 0)] if k in CUT else [(k, 0, cap, 1)]
        packed = pack(sep, chunks, chunk_turns, counts, above, cap, turns, True)
        slots = [turn_over(p, "sub", sub_count, t[0]) if t[0] else p for p, t in zip(packed, turns)]
        early = [n for n in range(len(turns)) if turns[n][3]]
        late = [n for n in range(len(turns)) if turns[n][2] > turns[n][1]]
        late.sort(key=lambda n: turn_order(sub_count, LATE_ORDER).index(turns[n][0]))
        above_places = [(i, turns[n][2] - turns[n][1], 0, kept, turns[n][0]) for i, n in enumerate(early)]
        places = [(i, 0, turns[n][1], turns[n][2], turns[n][0]) for i, n in enumerate(late)]
        early, late = [slots[n] for n in early], [slots[n] for n in late]
    else:
        regrouped = coefficients.reshape(vec_count, slice_cols, coefficients.shape[1])
        regrouped = lax.all_to_all(regrouped, "vec", split_axis=0, concat_axis=0, tiled=True)
        turns = [(k, 0, cap, 1) for k in range(sub_count)]
        slots = pack(sep, list(regrouped), list(range(vec_count)), counts, above, cap, turns, False)
        slots = lax.all_to_all(jnp.stack(slots), "sub", split_axis=0, concat_axis=0, tiled=True)
        early = late = [slots.reshape(group, cap + kept)]
        above_places, places = [(0, cap, 0, kept, None)], [(0, 0, 0, cap, None)]
    total, own = above_fields(early, above_places, group, sep, masked)
    return interior(late, places, group, count, interior_modes, total), own


def solution(mesh):
    placed = (P("sub", "vec"), P(), P(), P("sub", None), P(), P("sub", None), P("sub", None, None))
    return jax.shard_map(
        body,
        mesh=mesh,
        in_specs=placed,
        out_specs=(P("sub", "vec"), P("sub", "vec")),
        check_vma=False,
    )
```
